32 devices in a mesh: dp: 4 (over z), tensor: 8 (over y, x, core).
Axes of the slice: x: 2, y: 2, z: 4, core: 2. Of those that a mesh axis runs over, the one named last changes fastest.
Arguments:
- inputs: bfloat16 [4096, 1024], P('dp'), may hold values from -6 to 6
- conditioning: bfloat16 [4, 1024], P('dp'), may hold values from -6 to 6
- cotangent: bfloat16 [4096, 1024], P('dp'), may hold values from -6 to 6
- w_ada: float32 [1024, 6144], P('dp', 'tensor'), may hold values from -0.1875 to 0.1875
- w_qkv: float32 [1024, 3072], P('dp', 'tensor'), may hold values from -0.1875 to 0.1875
- w_proj: float32 [1024, 1024], P('tensor', 'dp'), may hold values from -1 to 1
- w_fc1: float32 [1024, 4096], P('dp', 'tensor'), may hold values from -0.1875 to 0.1875
- w_fc2: float32 [4096, 1024], P('tensor', 'dp'), may hold values from -0.09375 to 0.09375
- col_bias: float32 [12288], P(('tensor', 'dp')), may hold values from -1.2 to 1.2
- row_bias: float32 [2, 1024], P(None, 'dp'), may hold values from -1.2 to 1.2
- m_ada: float32 [1024, 6144], P('dp', 'tensor'), may hold values from -20 to 20
- v_ada: float32 [1024, 6144], P('dp', 'tensor'), may hold values from 30.72 to 307.2
- m_qkv: float32 [1024, 3072], P('dp', 'tensor'), may hold values from -40 to 40
- v_qkv: float32 [1024, 3072], P('dp', 'tensor'), may hold values from 122.88 to 1228.8
- m_proj: float32 [1024, 1024], P('tensor', 'dp'), may hold values from -4 to 4
- v_proj: float32 [1024, 1024], P('tensor', 'dp'), may hold values from 1.2288 to 12.288
- m_fc1: float32 [1024, 4096], P('dp', 'tensor'), may hold values from -20 to 20
- v_fc1: float32 [1024, 4096], P('dp', 'tensor'), may hold values from 30.72 to 307.2
- m_fc2: float32 [4096, 1024], P('tensor', 'dp'), may hold values from -20 to 20
- v_fc2: float32 [4096, 1024], P('tensor', 'dp'), may hold values from 30.72 to 307.2
- m_col: float32 [12288], P(('tensor', 'dp')), may hold values from -32 to 32
- v_col: float32 [12288], P(('tensor', 'dp')), may hold values from 60.2112 to 602.112
- m_row: float32 [2, 1024], P(None, 'dp'), may hold values from -32 to 32
- v_row: float32 [2, 1024], P(None, 'dp'), may hold values from 60.2112 to 602.112
Outputs:
- block_out: float32 [4096, 1024], P(('dp', 'tensor'))
- input_grad: float32 [4096, 1024], P(('dp', 'tensor'))
- cond_grad: float32 [4, 1024], P('dp', 'tensor')
- ada_grad: float32 [1024, 6144], P('dp', 'tensor')
- ada_second: float32 [1024, 6144], P('dp', 'tensor')
- ada_new: float32 [1024, 6144], P('dp', 'tensor')
- qkv_grad: float32 [1024, 3072], P('dp', 'tensor')
- qkv_second: float32 [1024, 3072], P('dp', 'tensor')
- qkv_new: float32 [1024, 3072], P('dp', 'tensor')
- proj_grad: float32 [1024, 1024], P('tensor', 'dp')
- proj_second: float32 [1024, 1024], P('tensor', 'dp')
- proj_new: float32 [1024, 1024], P('tensor', 'dp')
- fc1_grad: float32 [1024, 4096], P('dp', 'tensor')
- fc1_second: float32 [1024, 4096], P('dp', 'tensor')
- fc1_new: float32 [1024, 4096], P('dp', 'tensor')
- fc2_grad: float32 [4096, 1024], P('tensor', 'dp')
- fc2_second: float32 [4096, 1024], P('tensor', 'dp')
- fc2_new: float32 [4096, 1024], P('tensor', 'dp')
- col_grad: float32 [12288], P(('tensor', 'dp'))
- col_second: float32 [12288], P(('tensor', 'dp'))
- col_new: float32 [12288], P(('tensor', 'dp'))
- row_grad: float32 [2, 1024], P(None, 'dp')
- row_second: float32 [2, 1024], P(None, 'dp')
- row_new: float32 [2, 1024], P(None, 'dp')
The draws below stay inside these ranges and needn't reach their ends.
All inputs are finite; a program needn't handle non-finite values.
Results may differ from the reference program's by a relative error of at most 0.02.
The reference program's roundings to bfloat16 on the way count: a program that leaves them out, or rounds other values in their place, can miss the bound.
Values may be sent and summed in bfloat16 or wider, within the bound.
No kernel may reach another device: no remote copies, remote signals or barrier semaphores. Data moves between devices by JAX's collectives and lax.ppermute only.
A program may use at most 128 MiB of HBM per device.

```python
import math
import jax
import jax.numpy as jnp
from jax import lax

D = 1024
HEADS = 16
HD = 64
FF = 4096
SEQ = 1024
STEP = 10
ADA = 6144
CB = 12288
LATENTS = 4
TOKENS = 4096
N_TENSOR = 8


def block_scale(rng, shape, pieces, least, largest):
    loudness = 1.0
    for dim, blocks in pieces:
        steps = jax.random.uniform(jax.random.fold_in(jax.random.fold_in(rng, 6), dim), (blocks,), jnp.float32, least / len(pieces), largest / len(pieces))
        loudness = loudness * jnp.repeat(jnp.exp(steps), shape[dim] // blocks).reshape((-1,) + (1,) * (len(shape) - 1 - dim))
    return loudness


def noise(stream_key, extent, spread, limit, split=(), dtype=jnp.bfloat16):
    values = jax.random.normal(stream_key, extent, jnp.float32) * spread
    if len(split) > 0:
        values = block_scale(stream_key, extent, split, -0.22, 0.18) * values
    return jnp.clip(values, min=-limit, max=limit).astype(dtype)


def setup_inputs(seed: int = 0) -> dict:
    streams_of = jax.random.split(jax.random.key(seed), 25)
    return {
        "inputs": noise(streams_of[0], (TOKENS, D), 1.0, 6.0, ((0, 4),)),
        "conditioning": noise(streams_of[1], (LATENTS, D), 1.0, 6.0, ((0, 4),)),
        "cotangent": noise(streams_of[2], (TOKENS, D), 1.0, 6.0, ((0, 4),)),
        "w_ada": noise(streams_of[3], (D, ADA), D ** -0.5, 0.1875, ((0, 4), (1, 8)), jnp.float32),
        "w_qkv": noise(streams_of[4], (D, 3 * D), D ** -0.5, 0.1875, ((0, 4), (1, 8)), jnp.float32),
        "w_proj": noise(streams_of[5], (D, D), (D // 32) ** -0.5, 1.0, ((0, 8), (1, 4)), jnp.float32),
        "w_fc1": noise(streams_of[6], (D, FF), D ** -0.5, 0.1875, ((0, 4), (1, 8)), jnp.float32),
        "w_fc2": noise(streams_of[7], (FF, D), FF ** -0.5, 0.09375, ((0, 8), (1, 4)), jnp.float32),
        "col_bias": noise(streams_of[8], (CB,), 0.2, 1.2, ((0, 32),), jnp.float32),
        "row_bias": noise(streams_of[9], (2, D), 0.2, 1.2, ((1, 4),), jnp.float32),
        "m_ada": noise(streams_of[10], (D, ADA), (0.055 * TOKENS ** 0.5), 20.0, ((0, 4), (1, 8)), jnp.float32),
        "v_ada": jnp.clip(jnp.exp(math.log(307.2) - 2.3025852 * jax.random.uniform(streams_of[11], (D, ADA), jnp.float32) ** block_scale(streams_of[11], (D, ADA), ((0, 4), (1, 8)), -0.2, 0.2)), 30.72, 307.2),
        "m_qkv": noise(streams_of[12], (D, 3 * D), (0.11 * TOKENS ** 0.5), 40.0, ((0, 4), (1, 8)), jnp.float32),
        "v_qkv": jnp.clip(jnp.exp(math.log(1228.8) - 2.3025852 * jax.random.uniform(streams_of[13], (D, 3 * D), jnp.float32) ** block_scale(streams_of[13], (D, 3 * D), ((0, 4), (1, 8)), -0.2, 0.2)), 122.88, 1228.8),
        "m_proj": noise(streams_of[14], (D, D), (0.011 * TOKENS ** 0.5), 4.0, ((0, 8), (1, 4)), jnp.float32),
        "v_proj": jnp.clip(jnp.exp(math.log(12.288) - 2.3025851 * jax.random.uniform(streams_of[15], (D, D), jnp.float32) ** block_scale(streams_of[15], (D, D), ((0, 8), (1, 4)), -0.2, 0.2)), 1.2288, 12.288),
        "m_fc1": noise(streams_of[16], (D, FF), (0.055 * TOKENS ** 0.5), 20.0, ((0, 4), (1, 8)), jnp.float32),
        "v_fc1": jnp.clip(jnp.exp(math.log(307.2) - 2.3025852 * jax.random.uniform(streams_of[17], (D, FF), jnp.float32) ** block_scale(streams_of[17], (D, FF), ((0, 4), (1, 8)), -0.2, 0.2)), 30.72, 307.2),
        "m_fc2": noise(streams_of[18], (FF, D), (0.055 * TOKENS ** 0.5), 20.0, ((0, 8), (1, 4)), jnp.float32),
        "v_fc2": jnp.clip(jnp.exp(math.log(307.2) - 2.3025852 * jax.random.uniform(streams_of[19], (FF, D), jnp.float32) ** block_scale(streams_of[19], (FF, D), ((0, 8), (1, 4)), -0.2, 0.2)), 30.72, 307.2),
        "m_col": noise(streams_of[20], (CB,), (0.077 * TOKENS ** 0.5), 32.0, ((0, 32),), jnp.float32),
        "v_col": jnp.clip(jnp.exp(math.log(602.112) - 2.3025851 * jax.random.uniform(streams_of[21], (CB,), jnp.float32) ** block_scale(streams_of[21], (CB,), ((0, 32),), -0.2, 0.2)), 60.2112, 602.112),
        "m_row": noise(streams_of[22], (2, D), (0.077 * TOKENS ** 0.5), 32.0, ((1, 4),), jnp.float32),
        "v_row": jnp.clip(jnp.exp(math.log(602.112) - 2.3025851 * jax.random.uniform(streams_of[23], (2, D), jnp.float32) ** block_scale(streams_of[23], (2, D), ((1, 4),), -0.2, 0.2)), 60.2112, 602.112),
    }


HIGH = lax.Precision.HIGHEST
LN_EPS = 1e-06
BETA_ONE = 0.9
BETA_TWO = 0.95
ADAM_EPS = 1e-08
DECAY = 0.1
LR_SCALE = 2.0
LR_BIAS = 0.2

@jax.custom_vjp
def low(v):
    return lax.optimization_barrier(v.astype(jnp.bfloat16)).astype(jnp.float32)

@jax.custom_vjp
def low_back(v):
    return v

def low_keep(v):
    return (low(v), None)

def low_pass(kept, grad):
    return (grad,)

def back_keep(v):
    return (v, None)

def back_low(kept, grad):
    return (low(grad),)
low.defvjp(low_keep, low_pass)
low_back.defvjp(back_keep, back_low)

def matmul(left, right):
    return jnp.dot(left, right, precision=HIGH)

def normalize(values):
    center = values - lax.optimization_barrier(jnp.mean(values, -1, keepdims=True))
    return center * lax.rsqrt(lax.optimization_barrier(jnp.mean(center * center, -1, keepdims=True)) + LN_EPS)

def unpack_columns(column):
    blocks = column.reshape(N_TENSOR, -1)
    ada_cols = ADA // N_TENSOR
    head_cols = D // N_TENSOR
    bias_ada = blocks[:, :ada_cols].reshape(ADA)
    bias_query = blocks[:, ada_cols:ada_cols + head_cols].reshape(D)
    bias_value = blocks[:, ada_cols + head_cols:ada_cols + 2 * head_cols].reshape(D)
    bias_up = blocks[:, ada_cols + 2 * head_cols:].reshape(FF)
    return (bias_ada, bias_query, bias_value, bias_up)

def head_attend(block):
    queries, keyset, values = (block[0], block[1], block[2])
    scores = low_back(matmul(queries, keyset.T) * HD ** (-0.5))
    attn_prob = low(jax.nn.softmax(scores, axis=-1))
    return matmul(attn_prob, values)

def forward_latent(params, tokens_in, cond_row):
    ada_w, qkv_w, proj_w, up_w, down_w, column, rowvec = [low(weight) for weight in params]
    bias_ada, bias_query, bias_value, bias_up = unpack_columns(column)
    silu_cond = low(jax.nn.silu(cond_row))
    modulation = low_back(matmul(silu_cond[None], ada_w)[0] + bias_ada).reshape(6, D)
    normed1 = normalize(tokens_in)
    mod_in1 = low(normed1 * (1.0 + modulation[1]) + modulation[0])
    qkv_pre = matmul(mod_in1, qkv_w).reshape(SEQ, HEADS, 3, HD)
    bias_qkv = jnp.stack([bias_query.reshape(HEADS, HD), jnp.zeros((HEADS, HD), jnp.float32), bias_value.reshape(HEADS, HD)], axis=1)
    qkv_act = low(low_back(qkv_pre + bias_qkv))
    blocks = qkv_act.transpose(1, 2, 0, 3)
    heads_out = lax.map(jax.checkpoint(head_attend), blocks)
    attended = low(low_back(heads_out.transpose(1, 0, 2).reshape(SEQ, D)))
    branch1 = low_back(matmul(attended, proj_w) + rowvec[0])
    resid1 = tokens_in + modulation[2] * branch1
    normed2 = normalize(resid1)
    mod_in2 = low(normed2 * (1.0 + modulation[4]) + modulation[3])
    pre_act = low_back(matmul(mod_in2, up_w) + bias_up)
    activ = low(jax.nn.gelu(pre_act, approximate=True))
    branch2 = low_back(matmul(activ, down_w) + rowvec[1])
    return resid1 + modulation[5] * branch2

def adam_step(weight, first, second, grad, rate, decay):
    first_new = BETA_ONE * first + (1.0 - BETA_ONE) * grad
    second_new = BETA_TWO * second + (1.0 - BETA_TWO) * grad * grad
    fix_one = 1.0 - BETA_ONE ** STEP
    fix_two = 1.0 - BETA_TWO ** STEP
    step_dir = first_new / fix_one / (jnp.sqrt(second_new / fix_two) + ADAM_EPS)
    return (second_new, weight - rate * (step_dir + decay * weight))

def reference(inputs, conditioning, cotangent, w_ada, w_qkv, w_proj, w_fc1, w_fc2, col_bias, row_bias, m_ada, v_ada, m_qkv, v_qkv, m_proj, v_proj, m_fc1, v_fc1, m_fc2, v_fc2, m_col, v_col, m_row, v_row):
    tokens_all = inputs.astype(jnp.float32).reshape(LATENTS, SEQ, D)
    cond_all = conditioning.astype(jnp.float32)
    grad_out = cotangent.astype(jnp.float32).reshape(LATENTS, SEQ, D)
    params = (w_ada, w_qkv, w_proj, w_fc1, w_fc2, col_bias, row_bias)

    def latent_step(totals, item):
        tokens_in, cond_row, grad_row = item
        output, pullback = jax.vjp(forward_latent, params, tokens_in, cond_row)
        grad_params, grad_tokens, grad_cond = pullback(grad_row)
        totals = jax.tree.map(lambda first_arr, second_arr: first_arr + second_arr, totals, tuple(grad_params))
        return (totals, (output, grad_tokens, grad_cond))
    zeros_init = tuple((jnp.zeros_like(weight) for weight in params))
    grads, (outputs, grad_tokens, grad_cond) = lax.scan(latent_step, zeros_init, (tokens_all, cond_all, grad_out))
    ada_grad, qkv_grad, proj_grad, fc1_grad, fc2_grad, col_grad, row_grad = grads
    ada_second, ada_new = adam_step(w_ada, m_ada, v_ada, ada_grad, LR_SCALE * D ** (-0.5), DECAY)
    qkv_second, qkv_new = adam_step(w_qkv, m_qkv, v_qkv, qkv_grad, LR_SCALE * D ** (-0.5), DECAY)
    proj_second, proj_new = adam_step(w_proj, m_proj, v_proj, proj_grad, LR_SCALE * (D // 32) ** (-0.5), DECAY)
    fc1_second, fc1_new = adam_step(w_fc1, m_fc1, v_fc1, fc1_grad, LR_SCALE * D ** (-0.5), DECAY)
    fc2_second, fc2_new = adam_step(w_fc2, m_fc2, v_fc2, fc2_grad, LR_SCALE * FF ** (-0.5), DECAY)
    col_second, col_new = adam_step(col_bias, m_col, v_col, col_grad, LR_BIAS, 0.0)
    row_second, row_new = adam_step(row_bias, m_row, v_row, row_grad, LR_BIAS, 0.0)
    return (outputs.reshape(TOKENS, D), grad_tokens.reshape(TOKENS, D), grad_cond, ada_grad, ada_second, ada_new, qkv_grad, qkv_second, qkv_new, proj_grad, proj_second, proj_new, fc1_grad, fc1_second, fc1_new, fc2_grad, fc2_second, fc2_new, col_grad, col_second, col_new, row_grad, row_second, row_new)
```

```python
import functools

import jax
import jax.numpy as jnp
from jax import lax
from jax.experimental import pallas as pl
from jax.experimental.pallas import tpu as pltpu
from jax.sharding import PartitionSpec as P

HD = 64
STEP = 10
LN_EPS = 1e-06
GELU_C = 0.7978845608028654
GELU_K = 0.044715
BETA_ONE = 0.9
BETA_TWO = 0.95
ADAM_EPS = 1e-08
DECAY = 0.1
LR_SCALE = 2.0
LR_BIAS = 0.2
BF = jnp.bfloat16
F32 = jnp.float32
VMEM_LIMIT = 48 * 1024 * 1024


def dot(left, right, left_dim=1, right_dim=0):
    return lax.dot_general(
        left, right, (((left_dim,), (right_dim,)), ((), ())), preferred_element_type=F32
    )


def normalize(values):
    center = values - jnp.mean(values, -1, keepdims=True)
    inv_std = lax.rsqrt(jnp.mean(center * center, -1, keepdims=True) + LN_EPS)
    return (center * inv_std, inv_std)


def norm_back(grad_n, normed, inv_std):
    return inv_std * (
        grad_n
        - jnp.mean(grad_n, -1, keepdims=True)
        - normed * jnp.mean(grad_n * normed, -1, keepdims=True)
    )


def gelu_pair(values):
    square = values * values
    inner = GELU_C * (values + GELU_K * square * values)
    tanh_val = jnp.tanh(inner)
    half = 0.5 * (1.0 + tanh_val)
    result = values * half
    slope = half + 0.5 * values * (1.0 - tanh_val * tanh_val) * GELU_C * (
        1.0 + 3.0 * GELU_K * square
    )
    return (result, slope)


def full(shape):
    return pl.BlockSpec(shape, lambda *_: (0,) * len(shape))


def rows_of(count, width):
    return pl.BlockSpec((count, width), lambda i, *_: (i, 0))


def call(body, grid, in_specs, out_specs, out_shape, args, scratch=(), scalar=None, flops=0, nbytes=0):
    params = pltpu.CompilerParams(vmem_limit_bytes=VMEM_LIMIT)
    cost = pl.CostEstimate(flops=flops, bytes_accessed=nbytes, transcendentals=0)
    if scalar is None:
        return pl.pallas_call(
            body, grid=grid, in_specs=in_specs, out_specs=out_specs, out_shape=out_shape,
            scratch_shapes=list(scratch), compiler_params=params, cost_estimate=cost,
        )(*args)
    spec = pltpu.PrefetchScalarGridSpec(
        num_scalar_prefetch=1, grid=grid, in_specs=in_specs, out_specs=out_specs,
        scratch_shapes=list(scratch),
    )
    return pl.pallas_call(
        body, grid_spec=spec, out_shape=out_shape, compiler_params=params, cost_estimate=cost,
    )(scalar, *args)


def shape(dims, dtype):
    return jax.ShapeDtypeStruct(dims, dtype)


def enter_body(x_ref, mod_ref, w_ref, bias_ref, min_ref, qkv_ref):
    normed, _ = normalize(x_ref[...].astype(F32))
    low = (normed * (1.0 + mod_ref[1:2, :]) + mod_ref[0:1, :]).astype(BF)
    min_ref[...] = low
    width = qkv_ref.shape[1]
    qkv_ref[...] = (dot(low, w_ref[:, :width]) + bias_ref[...]).astype(BF)


def attend_body(blk_ref, qkv_ref, out_ref, lse_ref):
    heads = lse_ref.shape[0]
    outs = []
    blk = blk_ref[...]
    allr = qkv_ref[...]
    for h in range(heads):
        base = h * 3 * HD
        query = blk[:, base : base + HD]
        key = allr[:, base + HD : base + 2 * HD]
        value = allr[:, base + 2 * HD : base + 3 * HD]
        scores = dot(key, query, 1, 1) * HD ** (-0.5)
        highest = jnp.max(scores, 0, keepdims=True)
        expon = jnp.exp(scores - highest)
        totals = jnp.sum(expon, 0, keepdims=True)
        prob = (expon * (1.0 / totals)).astype(BF)
        outs.append(dot(value, prob, 0, 0).T.astype(BF))
        lse_ref[h : h + 1, :] = highest + jnp.log(totals)
    out_ref[...] = outs[0] if heads == 1 else jnp.concatenate(outs, axis=1)


def middle_body(count, rows, t_ref, *refs):
    att = refs[:count]
    (proj_ref, x_ref, mod_ref, bias_ref, min_ref, res_ref, nrm_ref, inv_ref, br_ref,
     res_s, nrm_s, inv_s, br_s) = refs[count:]
    block = x_ref.shape[0]
    joined = jnp.concatenate([r[...] for r in att], axis=1)
    branch = dot(joined, proj_ref[...], 1, 1) + bias_ref[...]
    resid = x_ref[...].astype(F32) + mod_ref[2:3, :] * branch
    normed, inv = normalize(resid)
    min_ref[...] = (normed * (1.0 + mod_ref[4:5, :]) + mod_ref[3:4, :]).astype(BF)
    start = t_ref[0] * rows
    step = pl.program_id(0)

    @pl.when(step == start // block)
    def _():
        res_s[...] = resid
        nrm_s[...] = normed
        inv_s[...] = jnp.broadcast_to(inv, inv_s.shape)
        br_s[...] = branch
        own = pl.ds(pl.multiple_of(start % block, rows), rows)
        res_ref[...] = res_s[own, :]
        nrm_ref[...] = nrm_s[own, :]
        inv_ref[...] = inv_s[own, :]
        br_ref[...] = br_s[own, :]


def store_pair(odd, value, rows, keep_ref, send_ref):
    low, high = value[:rows], value[rows:]
    keep_ref[0] = jnp.where(odd, high, low)
    send_ref[0] = jnp.where(odd, low, high)


def mlp_body(rows, t_ref, in_ref, cot_ref, mod_ref, w_ref, bias_ref,
             act_ref, dpre_ref, db_ref, keep_ref, send_ref, upsum_ref, downsum_ref):
    hidden = act_ref.shape[1]
    up = w_ref[:, :hidden]
    down_t = w_ref[:, hidden:]
    pre = dot(in_ref[...], up) + bias_ref[...]
    act, slope = gelu_pair(pre)
    act_ref[...] = act.astype(BF)
    grad_b = (cot_ref[...].astype(F32) * mod_ref[5:6, :]).astype(BF)
    db_ref[...] = grad_b
    dpre = (dot(grad_b, down_t) * slope).astype(BF)
    dpre_ref[...] = dpre
    part = dot(dpre, up, 1, 1).astype(BF)
    store_pair(t_ref[0] % 2 == 1, part, rows, keep_ref, send_ref)

    @pl.when(pl.program_id(0) == 0)
    def _():
        upsum_ref[...] = jnp.zeros_like(upsum_ref)
        downsum_ref[...] = jnp.zeros_like(downsum_ref)

    upsum_ref[...] += jnp.sum(dpre.astype(F32), 0, keepdims=True)
    downsum_ref[...] += jnp.sum(grad_b.astype(F32), 0, keepdims=True)


def down_body(rows, t_ref, act_ref, w_ref, keep_ref, send_ref):
    hidden = act_ref.shape[1]
    part = dot(act_ref[...], w_ref[:, hidden:], 1, 1).astype(BF)
    store_pair(t_ref[0] % 2 == 1, part, rows, keep_ref, send_ref)


def between_body(din_ref, nrm_ref, inv_ref, mod_ref, cot_ref, br_ref, dres_ref, dbr_ref, sums_ref):
    din = din_ref[...]
    normed = nrm_ref[...]
    inv = inv_ref[:, 0:1]
    dres = cot_ref[...].astype(F32) + norm_back(din * (1.0 + mod_ref[4:5, :]), normed, inv)
    dres_ref[...] = dres
    dbr_ref[...] = (mod_ref[2:3, :] * dres).astype(BF)
    sums_ref[0:1, :] = jnp.sum(dres * br_ref[...], 0, keepdims=True)
    sums_ref[1:2, :] = jnp.sum(din, 0, keepdims=True)
    sums_ref[2:3, :] = jnp.sum(din * normed, 0, keepdims=True)


def attend_back_body(count, rows, t_ref, *refs):
    dbr = refs[:count]
    w_ref, qkv_ref, lse_ref, out_ref, colsum_ref, projsum_ref, datt, acc = refs[count:]
    heads = lse_ref.shape[0]
    width = out_ref.shape[1]
    seq = qkv_ref.shape[0]
    block = lse_ref.shape[1]
    step = pl.program_id(0)
    scale = HD ** (-0.5)

    @pl.when(step == 0)
    def _():
        total = jnp.zeros(projsum_ref.shape, F32)
        for r in range(count):
            piece = dbr[r][...]
            at = pl.ds(pl.multiple_of((t_ref[0] ^ r) * rows, rows), rows)
            datt[at, :] = dot(piece, w_ref[:, width:]).astype(BF)
            total += jnp.sum(piece.astype(F32), 0, keepdims=True)
        projsum_ref[...] = total
        acc[...] = jnp.zeros_like(acc)

    here = pl.ds(pl.multiple_of(step * block, block), block)
    blk = qkv_ref[here, :]
    allr = qkv_ref[...]
    grads = datt[here, :]
    for h in range(heads):
        base = h * 3 * HD
        query = blk[:, base : base + HD]
        key = allr[:, base + HD : base + 2 * HD]
        value = allr[:, base + 2 * HD : base + 3 * HD]
        grad = grads[:, h * HD : (h + 1) * HD]
        scores = dot(key, query, 1, 1) * scale
        prob = jnp.exp(scores - lse_ref[h : h + 1, :])
        dprob = dot(value, grad, 1, 1)
        weighted = jnp.sum(prob * dprob, 0, keepdims=True)
        dscore = (prob * (dprob - weighted)).astype(BF)
        acc[3 * h, here, :] = dot(key, dscore, 0, 0).T * scale
        acc[3 * h + 1] += dot(dscore, query)
        acc[3 * h + 2] += dot(prob.astype(BF), grad)

    @pl.when(step == seq // block - 1)
    def _():
        parts = []
        for h in range(heads):
            parts += [acc[3 * h], acc[3 * h + 1] * scale, acc[3 * h + 2]]
        result = jnp.concatenate(parts, axis=1).astype(BF)
        out_ref[...] = result
        colsum_ref[...] = jnp.sum(result.astype(F32), 0, keepdims=True)


def leave_body(rows, t_ref, dqkv_ref, w_ref, x_ref, keep_ref, send_ref, sums_ref):
    width = dqkv_ref.shape[1]
    part = dot(dqkv_ref[...], w_ref[:, :width], 1, 1)
    store_pair(t_ref[0] % 2 == 1, part.astype(BF), rows, keep_ref, send_ref)
    normed, _ = normalize(x_ref[...].astype(F32))

    @pl.when(pl.program_id(0) == 0)
    def _():
        sums_ref[...] = jnp.zeros_like(sums_ref)

    sums_ref[0:1, :] += jnp.sum(part, 0, keepdims=True)
    sums_ref[1:2, :] += jnp.sum(part * normed, 0, keepdims=True)


def last_body(din_ref, x_ref, mod_ref, dres_ref, out_ref):
    normed, inv = normalize(x_ref[...].astype(F32))
    out_ref[...] = dres_ref[...] + norm_back(din_ref[...] * (1.0 + mod_ref[1:2, :]), normed, inv)


def adam_step(weight, first, second, grad, rate, decay):
    first_new = BETA_ONE * first + (1.0 - BETA_ONE) * grad
    second_new = BETA_TWO * second + (1.0 - BETA_TWO) * grad * grad
    fix_one = 1.0 - BETA_ONE**STEP
    fix_two = 1.0 - BETA_TWO**STEP
    step_dir = first_new / fix_one / (jnp.sqrt(second_new / fix_two) + ADAM_EPS)
    return (second_new, weight - rate * (step_dir + decay * weight))


def swap(value, mask, size):
    return lax.ppermute(value, "tensor", [(i, i ^ mask) for i in range(size)])


def spread(block, size):
    if size != 8:
        have = {0: block}
        bit = 1
        while bit < size:
            for r in list(have):
                have[r ^ bit] = swap(have[r], bit, size)
            bit *= 2
        return [have[r] for r in range(size)]
    half = block.shape[0] // 2
    by_x = swap(block, 2, size)
    by_y = swap(block, 4, size)
    core = swap(block, 1, size)
    diag_a = swap(by_x[:half], 4, size)
    diag_b = swap(by_y[half:], 2, size)
    core_x = swap(by_x, 1, size)
    core_y = swap(by_y, 1, size)
    diag = jnp.concatenate([diag_a, diag_b], axis=0)
    core_d = swap(diag, 1, size)
    return [block, core, by_x, core_x, by_y, core_y, diag, core_d]


def fold(keep, send, size):
    total = keep.astype(F32) + swap(send, 1, size).astype(F32)
    width = total.shape[-1]
    half = width // 2
    bits = []
    bit = 1
    while bit < size // 2:
        bits.append(bit)
        bit *= 2
    parts = []
    for cols, order in ((slice(0, half), bits), (slice(half, width), bits[::-1])):
        have = {m: total[m, :, cols] for m in range(size // 2)}
        parts.append((have, order))
    for stage in range(len(bits)):
        for have, order in parts:
            bit = order[stage]
            away = [m for m in sorted(have) if m & bit]
            moved = swap(jnp.stack([have[m] for m in away]).astype(BF), 2 * bit, size)
            for n, m in enumerate(away):
                have[m ^ bit] = have[m ^ bit] + moved[n].astype(F32)
                del have[m]
    return jnp.concatenate([have[0] for have, _ in parts], axis=1)


def shards(
    inputs, conditioning, cotangent, w_ada, w_qkv, w_proj, w_fc1, w_fc2, col_bias, row_bias,
    m_ada, v_ada, m_qkv, v_qkv, m_proj, v_proj, m_fc1, v_fc1, m_fc2, v_fc2, m_col, v_col, m_row, v_row,
):
    T = lax.axis_size("tensor")
    G = lax.axis_size("dp")
    t = lax.axis_index("tensor")
    z = lax.axis_index("dp")
    S, D = inputs.shape
    rows = S // T
    hc = w_proj.shape[0]
    heads = hc // HD
    F = w_fc1.shape[1]
    ada = w_ada.shape[1]
    share = D // G
    tid = t.astype(jnp.int32).reshape(1)

    def around(value, k):
        return lax.ppermute(value, "dp", [(i, (i + k) % G) for i in range(G)])

    first_all = lax.all_gather(
        jnp.concatenate([w_qkv.astype(BF), w_proj.astype(BF).T], axis=1), "dp", axis=0, tiled=True
    )
    mlp_all = lax.all_gather(
        jnp.concatenate([w_fc1.astype(BF), w_fc2.astype(BF).T], axis=1), "dp", axis=0, tiled=True
    )
    w_ada_low = w_ada.astype(BF)

    cond = conditioning.astype(F32)
    silu_low = (cond * jax.nn.sigmoid(cond)).astype(BF)
    small = jnp.concatenate([silu_low.reshape(-1), col_bias.astype(BF), row_bias.astype(BF).reshape(-1)])
    small_rel = jnp.stack([small] + [around(small, k) for k in range(1, G)])
    silu_rel = lax.dynamic_slice_in_dim(small_rel[:, :D], z * share, share, 1)
    bias_rev = small_rel[::-1, D:]
    bias_abs = lax.dynamic_slice_in_dim(
        jnp.concatenate([bias_rev, bias_rev], axis=0), G - 1 - z, G, 0
    ).astype(F32)
    n_col = col_bias.shape[0]
    cols = bias_abs[:, :n_col].reshape(-1)
    bias_rows = bias_abs[:, n_col:].reshape(G, 2, share).transpose(1, 0, 2).reshape(2, D)
    bias_ada = cols[:ada]
    bias_up = cols[ada + 2 * hc :].reshape(1, F)
    bias_qkv = jnp.stack(
        [cols[ada : ada + hc].reshape(heads, HD), jnp.zeros((heads, HD), F32),
         cols[ada + hc : ada + 2 * hc].reshape(heads, HD)], axis=1,
    ).reshape(1, 3 * hc)

    part = dot(silu_rel, w_ada_low)
    mod_part = part[0]
    for k in range(1, G):
        mod_part = mod_part + around(part[k], G - k)
    mod = lax.all_gather(mod_part + bias_ada, "tensor", axis=0, tiled=True).reshape(6, D)

    blk = min(256, S)
    steps = (S // blk,)
    mod_in1, qkv = call(
        enter_body, steps,
        [rows_of(blk, D), full((6, D)), full(first_all.shape), full((1, 3 * hc))],
        [rows_of(blk, D), rows_of(blk, 3 * hc)],
        [shape((S, D), BF), shape((S, 3 * hc), BF)],
        (inputs, mod, first_all, bias_qkv), flops=2 * S * D * 3 * hc, nbytes=6 * S * D,
    )
    attended, lse = call(
        attend_body, steps,
        [rows_of(blk, 3 * hc), full((S, 3 * hc))],
        [rows_of(blk, hc), pl.BlockSpec((heads, blk), lambda i: (0, i))],
        [shape((S, hc), BF), shape((heads, S), F32)],
        (qkv, qkv), flops=16 * S * S * hc, nbytes=4 * S * hc,
    )
    proj_rel = jnp.concatenate(spread(first_all[:, 3 * hc :], T), axis=1)
    att_rel = spread(attended, T)
    mod_in2, resid1, normed2, inv2, branch1 = call(
        functools.partial(middle_body, T, rows), steps,
        [rows_of(blk, hc)] * T + [full((D, D)), rows_of(blk, D), full((6, D)), full((1, D))],
        [rows_of(blk, D), full((rows, D)), full((rows, D)), full((rows, 128)), full((rows, D))],
        [shape((S, D), BF), shape((rows, D), F32), shape((rows, D), F32), shape((rows, 128), F32),
         shape((rows, D), F32)],
        (*att_rel, proj_rel, inputs, mod, bias_rows[0:1]),
        scratch=[pltpu.VMEM((blk, D), F32), pltpu.VMEM((blk, D), F32), pltpu.VMEM((blk, 128), F32),
                 pltpu.VMEM((blk, D), F32)],
        scalar=tid, flops=2 * S * D * D, nbytes=8 * S * D,
    )

    pair = 2 * rows
    pairs = (T // 2,)
    place = pl.BlockSpec((1, rows, D), lambda i, t_ref: (i ^ (t_ref[0] // 2), 0, 0))
    halves = [shape((T // 2, rows, D), BF)] * 2
    activ, dpre, dbranch2, keep, send, up_sum, down_sum = call(
        functools.partial(mlp_body, rows), pairs,
        [rows_of(pair, D), rows_of(pair, D), full((6, D)), full((D, 2 * F)), full((1, F))],
        [rows_of(pair, F), rows_of(pair, F), rows_of(pair, D), place, place, full((1, F)), full((1, D))],
        [shape((S, F), BF), shape((S, F), BF), shape((S, D), BF), *halves, shape((1, F), F32),
         shape((1, D), F32)],
        (mod_in2, cotangent, mod, mlp_all, bias_up), scalar=tid, flops=6 * S * D * F, nbytes=12 * S * D,
    )
    din2 = fold(keep, send, T)
    cot_rows = lax.dynamic_slice_in_dim(cotangent, t * rows, rows, 0)
    x_rows = lax.dynamic_slice_in_dim(inputs, t * rows, rows, 0)
    dres1, dbranch1, sums_mid = call(
        between_body, (1,),
        [full((rows, D)), full((rows, D)), full((rows, 128)), full((6, D)), full((rows, D)), full((rows, D))],
        [full((rows, D)), full((rows, D)), full((3, D))],
        [shape((rows, D), F32), shape((rows, D), BF), shape((3, D), F32)],
        (din2, normed2, inv2, mod, cot_rows, branch1), nbytes=24 * rows * D,
    )
    dbr_rel = spread(dbranch1, T)
    dqkv, qkv_sum, proj_sum = call(
        functools.partial(attend_back_body, T, rows), steps,
        [full((rows, D))] * T + [full(first_all.shape), full((S, 3 * hc)),
                                 pl.BlockSpec((heads, blk), lambda i, *_: (0, i))],
        [full((S, 3 * hc)), full((1, 3 * hc)), full((1, D))],
        [shape((S, 3 * hc), BF), shape((1, 3 * hc), F32), shape((1, D), F32)],
        (*dbr_rel, first_all, qkv, lse),
        scratch=[pltpu.VMEM((S, hc), BF), pltpu.VMEM((3 * heads, S, HD), F32)],
        scalar=tid, flops=40 * S * S * hc, nbytes=6 * S * D,
    )
    keep1, send1, sums_in = call(
        functools.partial(leave_body, rows), pairs,
        [rows_of(pair, 3 * hc), full(first_all.shape), rows_of(pair, D)],
        [place, place, full((2, D))],
        [*halves, shape((2, D), F32)],
        (dqkv, first_all, inputs), scalar=tid, flops=6 * S * D * hc, nbytes=6 * S * D,
    )
    din1 = fold(keep1, send1, T)
    input_grad = call(
        last_body, (1,),
        [full((rows, D)), full((rows, D)), full((6, D)), full((rows, D))],
        full((rows, D)), shape((rows, D), F32),
        (din1, x_rows, mod, dres1), nbytes=14 * rows * D,
    )

    keep2, send2 = call(
        functools.partial(down_body, rows), pairs,
        [rows_of(pair, F), full((D, 2 * F))],
        [place, place], halves, (activ, mlp_all), scalar=tid, flops=2 * S * D * F, nbytes=4 * S * D,
    )
    branch2 = fold(keep2, send2, T) + bias_rows[1:2]
    block_out = resid1 + mod[5:6] * branch2
    sums_out = jnp.sum(cot_rows.astype(F32) * branch2, 0, keepdims=True)

    mlp_grad = jnp.concatenate(
        [dot(mod_in2, dpre, 0, 0).astype(BF), dot(dbranch2, activ, 0, 0).astype(BF)], axis=1
    )
    mlp_grad = lax.psum_scatter(mlp_grad, "dp", scatter_dimension=0, tiled=True).astype(F32)
    att_rows = jnp.concatenate(
        [lax.dynamic_slice_in_dim(attended, (t ^ r) * rows, rows, 0) for r in range(T)], axis=0
    )
    first_grad = jnp.concatenate(
        [dot(mod_in1, dqkv, 0, 0).astype(BF),
         dot(jnp.concatenate(dbr_rel, axis=0), att_rows, 0, 0).astype(BF)], axis=1
    )
    first_grad = lax.psum_scatter(first_grad, "dp", scatter_dimension=0, tiled=True).astype(F32)

    dmod = jnp.concatenate([sums_in, sums_mid, sums_out], axis=0).reshape(T, ada)
    dmod = jnp.sum(lax.all_to_all(dmod, "tensor", 0, 0, tiled=True), 0)
    qkv_sum = qkv_sum.reshape(heads, 3, HD)
    message = jnp.concatenate(
        [dmod.astype(BF).astype(F32), qkv_sum[:, 0].reshape(-1), qkv_sum[:, 2].reshape(-1),
         up_sum.reshape(-1), proj_sum.reshape(-1), down_sum.reshape(-1)]
    )
    message_rel = jnp.stack([message] + [around(message, k) for k in range(1, G)])
    dmod_rel = message_rel[:, :ada].astype(BF)
    bias_sum = jnp.sum(message_rel, 0)
    col_sum = lax.dynamic_slice_in_dim(bias_sum[: G * n_col], z * n_col, n_col, 0)
    row_sum = lax.dynamic_slice_in_dim(bias_sum[G * n_col :].reshape(2, D), z * share, share, 1)
    ada_sum = dot(silu_rel, dmod_rel, 0, 0)
    per = T // G
    grad_silu = dot(dmod_rel, w_ada_low, 1, 1).reshape(T, D // T)
    grad_silu = jnp.sum(lax.all_to_all(grad_silu, "tensor", 0, 0, tiled=True), 0, keepdims=True)
    grad_silu = lax.ppermute(
        grad_silu, ("dp", "tensor"),
        [(a * T + b, ((a - b // per) % G) * T + a * per + b % per) for a in range(G) for b in range(T)],
    )
    cond_here = lax.dynamic_slice_in_dim(cond, t * (D // T), D // T, 1)
    sig_here = jax.nn.sigmoid(cond_here)
    cond_grad = grad_silu * sig_here * (1.0 + cond_here * (1.0 - sig_here))

    qkv_sum = first_grad[:, : 3 * hc]
    proj_sum = first_grad[:, 3 * hc :].T
    fc1_sum = mlp_grad[:, :F]
    fc2_sum = mlp_grad[:, F:].T
    hidden = F * T
    ada_second, ada_new = adam_step(w_ada, m_ada, v_ada, ada_sum, LR_SCALE * D ** (-0.5), DECAY)
    qkv_second, qkv_new = adam_step(w_qkv, m_qkv, v_qkv, qkv_sum, LR_SCALE * D ** (-0.5), DECAY)
    proj_second, proj_new = adam_step(
        w_proj, m_proj, v_proj, proj_sum, LR_SCALE * (D // 32) ** (-0.5), DECAY
    )
    fc1_second, fc1_new = adam_step(w_fc1, m_fc1, v_fc1, fc1_sum, LR_SCALE * D ** (-0.5), DECAY)
    fc2_second, fc2_new = adam_step(w_fc2, m_fc2, v_fc2, fc2_sum, LR_SCALE * hidden ** (-0.5), DECAY)
    col_second, col_new = adam_step(col_bias, m_col, v_col, col_sum, LR_BIAS, 0.0)
    row_second, row_new = adam_step(row_bias, m_row, v_row, row_sum, LR_BIAS, 0.0)
    return (
        block_out, input_grad, cond_grad,
        ada_sum, ada_second, ada_new,
        qkv_sum, qkv_second, qkv_new,
        proj_sum, proj_second, proj_new,
        fc1_sum, fc1_second, fc1_new,
        fc2_sum, fc2_second, fc2_new,
        col_sum, col_second, col_new,
        row_sum, row_second, row_new,
    )


def solution(mesh):
    by_cols = P("dp", "tensor")
    by_rows = P("tensor", "dp")
    column = P(("tensor", "dp"))
    row = P(None, "dp")
    tokens = P("dp", None)
    weights = (by_cols, by_cols, by_rows, by_cols, by_rows, column, row)
    moments = tuple(spec for spec in weights for _ in range(2))
    results = tuple(spec for spec in weights for _ in range(3))
    mine = P(("dp", "tensor"), None)
    return jax.shard_map(
        shards,
        mesh=mesh,
        in_specs=(tokens, tokens, tokens, *weights, *moments),
        out_specs=(mine, mine, by_cols, *results),
        check_vma=False,
    )
```

```python
import functools

import jax
import jax.numpy as jnp
from jax import lax
from jax.experimental import pallas as pl
from jax.experimental.pallas import tpu as pltpu
from jax.sharding import PartitionSpec as P

HD = 64
STEP = 10
LN_EPS = 1e-06
GELU_C = 0.7978845608028654
GELU_K = 0.044715
BETA_ONE = 0.9
BETA_TWO = 0.95
ADAM_EPS = 1e-08
DECAY = 0.1
LR_SCALE = 2.0
LR_BIAS = 0.2
BF = jnp.bfloat16
F32 = jnp.float32
MIB = 1024 * 1024


def dot(left, right, left_dim=1, right_dim=0):
    return lax.dot_general(
        left, right, (((left_dim,), (right_dim,)), ((), ())), preferred_element_type=F32
    )


def normalize(values):
    center = values - jnp.mean(values, -1, keepdims=True)
    inv_std = lax.rsqrt(jnp.mean(center * center, -1, keepdims=True) + LN_EPS)
    return (center * inv_std, inv_std)


def norm_back(grad_n, normed, inv_std):
    return inv_std * (
        grad_n
        - jnp.mean(grad_n, -1, keepdims=True)
        - normed * jnp.mean(grad_n * normed, -1, keepdims=True)
    )


def gelu_pair(values):
    square = values * values
    inner = GELU_C * (values + GELU_K * square * values)
    tanh_val = jnp.tanh(inner)
    half = 0.5 * (1.0 + tanh_val)
    result = values * half
    slope = half + 0.5 * values * (1.0 - tanh_val * tanh_val) * GELU_C * (
        1.0 + 3.0 * GELU_K * square
    )
    return (result, slope)


def full(shape):
    return pl.BlockSpec(shape, lambda *_: (0,) * len(shape))


def rows_of(count, width):
    return pl.BlockSpec((count, width), lambda i, *_: (i, 0))


def call(body, grid, in_specs, out_specs, out_shape, args, scratch=(), scalar=None, flops=0, nbytes=0, near=False):
    params = pltpu.CompilerParams(vmem_limit_bytes=(16 if near else 56) * MIB)
    cost = pl.CostEstimate(flops=flops, bytes_accessed=nbytes, transcendentals=0)
    if near:
        args = [pltpu.with_memory_space_constraint(a, pltpu.VMEM) for a in args]
    if scalar is None:
        return pl.pallas_call(
            body, grid=grid, in_specs=in_specs, out_specs=out_specs, out_shape=out_shape,
            scratch_shapes=list(scratch), compiler_params=params, cost_estimate=cost,
        )(*args)
    spec = pltpu.PrefetchScalarGridSpec(
        num_scalar_prefetch=1, grid=grid, in_specs=in_specs, out_specs=out_specs,
        scratch_shapes=list(scratch),
    )
    return pl.pallas_call(
        body, grid_spec=spec, out_shape=out_shape, compiler_params=params, cost_estimate=cost,
    )(scalar, *args)


def far_shape(dims, dtype):
    return pltpu.HBM(dims, dtype)


def shape(dims, dtype):
    return jax.ShapeDtypeStruct(dims, dtype)


def mod_body(count, s_ref, *refs):
    small = refs[:count]
    w_ref, part_ref, silu_ref, low_ref = refs[count:]
    share = w_ref.shape[0]
    at = pl.ds(pl.multiple_of(s_ref[1] * share, share), share)
    low = w_ref[...].astype(BF)
    silu = jnp.concatenate([r[:, at] for r in small], axis=0).astype(BF)
    low_ref[...] = low
    silu_ref[...] = silu
    part_ref[...] = dot(silu, low)


def pack_first_body(qkv_ref, proj_ref, out_ref):
    width = qkv_ref.shape[1]
    out_ref[:, :width] = qkv_ref[...].astype(BF)
    out_ref[:, width:] = proj_ref[...].T.astype(BF)


def pack_body(up_ref, down_ref, out_ref):
    share, hidden = up_ref.shape
    for n in range(hidden // share):
        out_ref[n * share : (n + 1) * share, :] = up_ref[:, n * share : (n + 1) * share].astype(BF)
    out_ref[hidden:, :] = down_ref[...].astype(BF)


def unpack_first_body(first_ref, w_ref, proj_ref):
    width = w_ref.shape[1]
    w_ref[...] = first_ref[:, :width]
    proj_ref[...] = first_ref[:, width:].T


def enter_body(x_ref, mod_ref, bias_ref, w_ref, min_ref, qkv_ref):
    normed, _ = normalize(x_ref[...].astype(F32))
    low = (normed * (1.0 + mod_ref[1:2, :]) + mod_ref[0:1, :]).astype(BF)
    min_ref[...] = low
    qkv_ref[...] = (dot(low, w_ref[...]) + bias_ref[...]).astype(BF)


def attend_body(blk_ref, qkv_ref, out_ref, lse_ref):
    heads = lse_ref.shape[0]
    outs = []
    blk = blk_ref[...]
    allr = qkv_ref[...]
    for h in range(heads):
        base = h * 3 * HD
        query = blk[:, base : base + HD] * BF(HD ** (-0.5))
        key = allr[:, base + HD : base + 2 * HD]
        value = allr[:, base + 2 * HD : base + 3 * HD]
        scores = dot(key, query, 1, 1)
        highest = jnp.max(scores, 0, keepdims=True)
        expon = jnp.exp(scores - highest)
        totals = jnp.sum(expon, 0, keepdims=True)
        out = dot(value, expon.astype(BF), 0, 0) * (1.0 / totals)
        outs.append(out.T.astype(BF))
        lse_ref[h : h + 1, :] = highest + jnp.log(totals)
    out_ref[...] = outs[0] if heads == 1 else jnp.concatenate(outs, axis=1)


def middle_body(count, rows, s_ref, *refs):
    att = refs[:count]
    proj = refs[count : 2 * count]
    x_ref, mod_ref, bias_ref, min_ref, br_ref, proj_s, br_s = refs[2 * count :]
    block = x_ref.shape[0]
    step = pl.program_id(0)

    @pl.when(step == 0)
    def _():
        at = 0
        for ref in proj:
            proj_s[at : at + ref.shape[0], :] = ref[...]
            at += ref.shape[0]

    joined = jnp.concatenate([ref[...] for ref in att], axis=1)
    branch = dot(joined, proj_s[...]) + bias_ref[...]
    resid = x_ref[...].astype(F32) + mod_ref[2:3, :] * branch
    normed, _ = normalize(resid)
    min_ref[...] = (normed * (1.0 + mod_ref[4:5, :]) + mod_ref[3:4, :]).astype(BF)
    start = s_ref[0] * rows

    @pl.when(step == start // block)
    def _():
        br_s[...] = branch
        br_ref[...] = br_s[pl.ds(pl.multiple_of(start % block, rows), rows), :]


def store_pair(odd, value, rows, keep_ref, send_ref):
    low, high = value[:rows], value[rows:]
    keep_ref[0] = jnp.where(odd, high, low)
    send_ref[0] = jnp.where(odd, low, high)


def mlp_body(rows, s_ref, in_ref, cot_ref, mod_ref, bias_ref, pack_ref,
             act_ref, dpre_ref, keep_ref, send_ref, keep2_ref, send2_ref, upsum_ref, downsum_ref, outsum_ref,
             down_s, up_s):
    planes, _, share = pack_ref.shape
    hidden = act_ref.shape[1]

    @pl.when(pl.program_id(0) == 0)
    def _():
        for plane in range(planes):
            at = slice(plane * share, (plane + 1) * share)
            for n in range(hidden // share):
                up_s[at, n * share : (n + 1) * share] = pack_ref[plane, n * share : (n + 1) * share, :]
            down_s[:, at] = pack_ref[plane, hidden:, :]
        upsum_ref[...] = jnp.zeros_like(upsum_ref)
        downsum_ref[...] = jnp.zeros_like(downsum_ref)
        outsum_ref[...] = jnp.zeros_like(outsum_ref)

    up = up_s[...]
    down = down_s[...]
    odd = s_ref[0] % 2 == 1
    cot = cot_ref[...].astype(F32)
    pre = dot(in_ref[...], up) + bias_ref[...]
    act, slope = gelu_pair(pre)
    act = act.astype(BF)
    act_ref[...] = act
    grad_b = (cot * mod_ref[5:6, :]).astype(BF)
    dpre = (dot(grad_b, down, 1, 1) * slope).astype(BF)
    dpre_ref[...] = dpre
    store_pair(odd, dot(dpre, up, 1, 1).astype(BF), rows, keep_ref, send_ref)
    part = dot(act, down)
    store_pair(odd, part.astype(BF), rows, keep2_ref, send2_ref)
    outsum_ref[...] += jnp.sum(cot * part, 0, keepdims=True)
    upsum_ref[...] += jnp.sum(dpre.astype(F32), 0, keepdims=True)
    downsum_ref[...] += jnp.sum(grad_b.astype(F32), 0, keepdims=True)


def mlp_grad_body(in_ref, dpre_ref, act_ref, cot_ref, mod_ref, out_ref):
    hidden = act_ref.shape[1]
    share = in_ref.shape[1]
    up = dot(in_ref[...], dpre_ref[...], 0, 0).astype(BF)
    for n in range(hidden // share):
        out_ref[0, n * share : (n + 1) * share, :] = up[:, n * share : (n + 1) * share]
    grad_b = (cot_ref[...].astype(F32) * mod_ref[5:6, :]).astype(BF)
    out_ref[0, hidden:, :] = dot(act_ref[...], grad_b, 0, 0).astype(BF)


def first_grad_body(s_ref, in_ref, dqkv_ref, proj_ref, out_ref):
    width = dqkv_ref.shape[1]
    out_ref[0, :, :width] = dot(in_ref[...], dqkv_ref[...], 0, 0).astype(BF)
    out_ref[0, :, width:] = proj_ref[...]


def split_left(total, keep_ref, send_ref):
    for n in range(keep_ref.shape[0]):
        keep_ref[n] = total[2 * n]
        send_ref[n] = total[2 * n + 1].astype(BF)


def split_right(total, keep_ref, send_ref):
    count = keep_ref.shape[0]
    for n in range(count):
        keep_ref[n] = total[n]
        send_ref[n] = total[count + n].astype(BF)


def fold_first_body(keep_ref, got_ref, lk_ref, ls_ref, rk_ref, rs_ref):
    half = lk_ref.shape[2]
    total = keep_ref[...].astype(F32) + got_ref[...].astype(F32)
    split_left(total[:, :, :half], lk_ref, ls_ref)
    split_right(total[:, :, half:], rk_ref, rs_ref)


def fold_next_body(left_ref, lgot_ref, right_ref, rgot_ref, lk_ref, ls_ref, rk_ref, rs_ref):
    split_left(left_ref[...] + lgot_ref[...].astype(F32), lk_ref, ls_ref)
    split_right(right_ref[...] + rgot_ref[...].astype(F32), rk_ref, rs_ref)


def fold_last(refs):
    left, lgot, right, rgot = refs
    return jnp.concatenate(
        [left[0] + lgot[0].astype(F32), right[0] + rgot[0].astype(F32)], axis=1
    )


def between_body(*refs):
    x_ref, mod_ref, cot_ref, br_ref, dres_ref, dbr_ref, res_ref, sums_ref = refs[4:]
    din = fold_last(refs[:4])
    resid = x_ref[...].astype(F32) + mod_ref[2:3, :] * br_ref[...]
    res_ref[...] = resid
    normed, inv = normalize(resid)
    dres = cot_ref[...].astype(F32) + norm_back(din * (1.0 + mod_ref[4:5, :]), normed, inv)
    dres_ref[...] = dres
    dbr_ref[...] = (mod_ref[2:3, :] * dres).astype(BF)
    sums_ref[0:1, :] = jnp.sum(dres * br_ref[...], 0, keepdims=True)
    sums_ref[1:2, :] = jnp.sum(din, 0, keepdims=True)
    sums_ref[2:3, :] = jnp.sum(din * normed, 0, keepdims=True)


def output_body(*refs):
    bias_ref, res_ref, mod_ref, out_ref = refs[4:]
    branch = fold_last(refs[:4]) + bias_ref[...]
    out_ref[...] = res_ref[...] + mod_ref[5:6, :] * branch


def attend_back_body(count, rows, s_ref, *refs):
    dbr = refs[:count]
    (proj_ref, qkv_ref, lse_ref, att_ref, out_ref, colsum_ref, projsum_ref, projgrad_ref,
     datt, acc) = refs[count:]
    heads = lse_ref.shape[0]
    seq = qkv_ref.shape[0]
    block = lse_ref.shape[1]
    step = pl.program_id(0)

    @pl.when(step == 0)
    def _():
        total = jnp.zeros(projsum_ref.shape, F32)
        grad = jnp.zeros(projgrad_ref.shape, F32)
        for r in range(count):
            block_in = dbr[r][...]
            at = pl.ds(pl.multiple_of((s_ref[0] ^ r) * rows, rows), rows)
            datt[at, :] = dot(block_in, proj_ref[...], 1, 1).astype(BF)
            total += jnp.sum(block_in.astype(F32), 0, keepdims=True)
            grad += dot(block_in, att_ref[at, :], 0, 0)
        projgrad_ref[...] = grad.astype(BF)
        projsum_ref[...] = total
        acc[...] = jnp.zeros_like(acc)

    here = pl.ds(pl.multiple_of(step * block, block), block)
    blk = qkv_ref[here, :]
    allr = qkv_ref[...]
    grads = datt[here, :]
    for h in range(heads):
        base = h * 3 * HD
        query = blk[:, base : base + HD] * BF(HD ** (-0.5))
        key = allr[:, base + HD : base + 2 * HD]
        value = allr[:, base + 2 * HD : base + 3 * HD]
        grad = grads[:, h * HD : (h + 1) * HD]
        prob = jnp.exp(dot(key, query, 1, 1) - lse_ref[h : h + 1, :])
        dprob = dot(value, grad, 1, 1)
        weighted = jnp.sum(prob * dprob, 0, keepdims=True)
        dscore = (prob * (dprob - weighted)).astype(BF)
        acc[3 * h, here, :] = dot(key, dscore, 0, 0).T * HD ** (-0.5)
        acc[3 * h + 1] += dot(dscore, query)
        acc[3 * h + 2] += dot(prob.astype(BF), grad)

    @pl.when(step == seq // block - 1)
    def _():
        result = jnp.concatenate([acc[n] for n in range(3 * heads)], axis=1).astype(BF)
        out_ref[...] = result
        colsum_ref[...] = jnp.sum(result.astype(F32), 0, keepdims=True)


def leave_body(rows, s_ref, dqkv_ref, w_ref, x_ref, keep_ref, send_ref, sums_ref):
    part = dot(dqkv_ref[...], w_ref[...], 1, 1)
    store_pair(s_ref[0] % 2 == 1, part.astype(BF), rows, keep_ref, send_ref)
    normed, _ = normalize(x_ref[...].astype(F32))

    @pl.when(pl.program_id(0) == 0)
    def _():
        sums_ref[...] = jnp.zeros_like(sums_ref)

    sums_ref[0:1, :] += jnp.sum(part, 0, keepdims=True)
    sums_ref[1:2, :] += jnp.sum(part * normed, 0, keepdims=True)


def last_body(*refs):
    x_ref, mod_ref, dres_ref, out_ref = refs[4:]
    normed, inv = normalize(x_ref[...].astype(F32))
    din = fold_last(refs[:4])
    out_ref[...] = dres_ref[...] + norm_back(din * (1.0 + mod_ref[1:2, :]), normed, inv)


def adam_step(weight, first, second, grad, rate, decay):
    first_new = BETA_ONE * first + (1.0 - BETA_ONE) * grad
    second_new = BETA_TWO * second + (1.0 - BETA_TWO) * grad * grad
    fix_one = 1.0 - BETA_ONE**STEP
    fix_two = 1.0 - BETA_TWO**STEP
    step_dir = first_new / fix_one / (jnp.sqrt(second_new / fix_two) + ADAM_EPS)
    return (second_new, weight - rate * (step_dir + decay * weight))


def adam_store(grad, w_ref, m_ref, v_ref, grad_ref, second_ref, new_ref, rate):
    grad_ref[...] = grad
    second, new = adam_step(w_ref[...], m_ref[...], v_ref[...], grad, rate, DECAY)
    second_ref[...] = second
    new_ref[...] = new


def adam_first_body(count, rate_qkv, rate_proj, *refs):
    width = refs[count].shape[1]
    grad = refs[0][...].astype(F32)
    for k in range(1, count):
        grad += refs[k][...].astype(F32)
    args, outs = refs[count : count + 6], refs[count + 6 :]
    adam_store(grad[:, :width], *args[:3], *outs[:3], rate_qkv)
    adam_store(grad[:, width:].T, *args[3:], *outs[3:], rate_proj)


def adam_ada_body(rate, silu_ref, dmod_ref, *refs):
    adam_store(dot(silu_ref[...], dmod_ref[...], 0, 0), *refs, rate)


def adam_mlp_body(rate_up, rate_down, gup_ref, gdown_ref, *refs):
    adam_store(gup_ref[...].astype(F32), *refs[0:3], *refs[6:9], rate_up)
    adam_store(gdown_ref[...].astype(F32), *refs[3:6], *refs[9:12], rate_down)


def swap(value, mask, size):
    return lax.ppermute(value, "tensor", [(i, i ^ mask) for i in range(size)])


def spread_first(block, size):
    return swap(block, 2, size), swap(block, 4, size), swap(block, 1, size)


def spread_second(near, size):
    by_x, by_y, _ = near
    return swap(by_x, 4, size), swap(by_x, 1, size), swap(by_y, 1, size)


def spread_third(block, near, more, size):
    by_x, by_y, core = near
    diag, core_x, core_y = more
    return [block, core, by_x, core_x, by_y, core_y, diag, swap(diag, 1, size)]


def spread(block, size):
    if size == 8:
        near = spread_first(block, size)
        return spread_third(block, near, spread_second(near, size), size)
    have = {0: block}
    bit = 1
    while bit < size:
        for r in list(have):
            have[r ^ bit] = swap(have[r], bit, size)
        bit *= 2
    return [have[r] for r in range(size)]


def fold(keep, send, size, beside=None):
    got = swap(send, 1, size)
    count, rows, width = keep.shape
    half = width // 2
    left = right = None
    stage = 0
    while count > 1:
        count //= 2
        dims = (count, rows, half)
        outs = [shape(dims, F32), shape(dims, BF)] * 2
        specs = [full(dims)] * 4
        if left is None:
            args, body = (keep, got), fold_first_body
        else:
            args, body = (left, lgot, right, rgot), fold_next_body
        left, lsend, right, rsend = call(
            body, (1,), [full(a.shape) for a in args], specs, outs, args,
            nbytes=20 * count * rows * width, near=True,
        )
        lgot = swap(lsend, 2 << stage, size)
        rgot = swap(rsend, (size // 2) >> stage, size)
        if beside is not None and stage == 0:
            done = beside(left)
            left, lgot, right, rgot, done = lax.optimization_barrier((left, lgot, right, rgot, done))
        stage += 1
    if beside is not None:
        return (left, lgot, right, rgot), done
    return left, lgot, right, rgot


def shards(
    inputs, conditioning, cotangent, w_ada, w_qkv, w_proj, w_fc1, w_fc2, col_bias, row_bias,
    m_ada, v_ada, m_qkv, v_qkv, m_proj, v_proj, m_fc1, v_fc1, m_fc2, v_fc2, m_col, v_col, m_row, v_row,
):
    T = lax.axis_size("tensor")
    G = lax.axis_size("dp")
    t = lax.axis_index("tensor")
    z = lax.axis_index("dp")
    S, D = inputs.shape
    rows = S // T
    hc = w_proj.shape[0]
    heads = hc // HD
    F = w_fc1.shape[1]
    ada = w_ada.shape[1]
    share = D // G
    scalar = jnp.stack([t, z]).astype(jnp.int32)
    n_col = col_bias.shape[0]

    def around(value, k):
        return lax.ppermute(value, "dp", [(i, (i + k) % G) for i in range(G)])

    def from_planes(value):
        return [value] + [around(value, k) for k in range(1, G)]

    first = call(
        pack_first_body, (1,), [full((share, 3 * hc)), full((hc, share))], full((share, 4 * hc)),
        shape((share, 4 * hc), BF), (w_qkv, w_proj), nbytes=24 * hc * share,
    )
    pack = call(
        pack_body, (1,), [full((share, F)), full((F, share))], full((2 * F, share)),
        shape((2 * F, share), BF), (w_fc1, w_fc2), nbytes=12 * F * share,
    )
    first_all = lax.all_gather(first, "dp", axis=0, tiled=True)
    pack_all = lax.all_gather(pack, "dp", axis=0, tiled=False)

    cond = conditioning.astype(F32)
    silu = (cond * jax.nn.sigmoid(cond)).astype(BF).astype(F32)
    small = jnp.concatenate(
        [silu, col_bias.astype(BF).astype(F32).reshape(1, -1), row_bias.astype(BF).astype(F32).reshape(1, -1)],
        axis=1,
    )
    small_rel = from_planes(small)
    part, silu_own, ada_low = call(
        functools.partial(mod_body, G), (1,),
        [full(small.shape)] * G + [full((share, ada))],
        [full((G, ada)), full((G, share)), full((share, ada))],
        [shape((G, ada), F32), shape((G, share), BF), shape((share, ada), BF)],
        (*small_rel, w_ada), scalar=scalar, nbytes=8 * share * ada, near=True,
    )
    bias_rev = jnp.concatenate(small_rel[::-1] * 2, axis=0)[:, D:]
    bias_abs = lax.dynamic_slice_in_dim(bias_rev, G - 1 - z, G, 0)
    cols = bias_abs[:, :n_col].reshape(-1)
    bias_rows = bias_abs[:, n_col:].reshape(G, 2, share).transpose(1, 0, 2).reshape(2, D)
    bias_up = cols[ada + 2 * hc :].reshape(1, F)
    bias_qkv = jnp.stack(
        [cols[ada : ada + hc].reshape(heads, HD), jnp.zeros((heads, HD), F32),
         cols[ada + hc : ada + 2 * hc].reshape(heads, HD)], axis=1,
    ).reshape(1, 3 * hc)
    mod_part = part[0:1] + cols[:ada].reshape(1, ada)
    for k in range(1, G):
        mod_part = mod_part + around(part[k : k + 1], G - k)
    mod = lax.all_gather(mod_part, "tensor", axis=1, tiled=True).reshape(6, D)

    first_all, mod = lax.optimization_barrier((first_all, mod))
    w_qkv_all, proj_own = call(
        unpack_first_body, (1,), [full((D, 4 * hc))],
        [full((D, 3 * hc)), full((hc, D))], [shape((D, 3 * hc), BF), shape((hc, D), BF)],
        (first_all,), nbytes=20 * hc * D,
    )

    blk = min(256, S)
    steps = (S // blk,)
    mod_in1, qkv = call(
        enter_body, steps,
        [rows_of(blk, D), full((6, D)), full((1, 3 * hc)), full((D, 3 * hc))],
        [rows_of(blk, D), rows_of(blk, 3 * hc)],
        [far_shape((S, D), BF), shape((S, 3 * hc), BF)],
        (inputs, mod, bias_qkv, w_qkv_all), flops=2 * S * D * 3 * hc, nbytes=6 * S * D,
    )
    attended, lse = call(
        attend_body, steps,
        [rows_of(blk, 3 * hc), full((S, 3 * hc))],
        [rows_of(blk, hc), pl.BlockSpec((heads, blk), lambda i: (0, i))],
        [shape((S, hc), BF), shape((heads, S), F32)],
        (qkv, qkv), flops=16 * S * S * hc, nbytes=4 * S * hc,
    )
    if T == 8:
        proj_near, _ = lax.optimization_barrier((spread_first(proj_own, T), qkv))
        proj_more, attended = lax.optimization_barrier((spread_second(proj_near, T), attended))
        proj_all = spread_third(proj_own, proj_near, proj_more, T)
    else:
        proj_all = spread(proj_own, T)
    att_rel = spread(attended, T)
    mod_in2, branch1 = call(
        functools.partial(middle_body, T, rows), steps,
        [rows_of(blk, hc)] * T + [full((hc, D))] * T + [rows_of(blk, D), full((6, D)), full((1, D))],
        [rows_of(blk, D), full((rows, D))],
        [far_shape((S, D), BF), shape((rows, D), F32)],
        (*att_rel, *proj_all, inputs, mod, bias_rows[0:1]),
        scratch=[pltpu.VMEM((T * hc, D), BF), pltpu.VMEM((blk, D), F32)],
        scalar=scalar, flops=2 * S * D * D, nbytes=8 * S * D,
    )

    pair = 2 * rows
    pairs = (T // 2,)
    place_pair = pl.BlockSpec((1, rows, D), lambda i, s_ref: (i ^ (s_ref[0] // 2), 0, 0))
    halves = [shape((T // 2, rows, D), BF)] * 2
    activ, dpre, keep, send, keep2, send2, up_sum, down_sum, out_sum = call(
        functools.partial(mlp_body, rows), pairs,
        [rows_of(pair, D), rows_of(pair, D), full((6, D)), full((1, F))]
        + [full((G, 2 * F, share))],
        [rows_of(pair, F), rows_of(pair, F)] + [place_pair] * 4 + [full((1, F)), full((1, D)), full((1, D))],
        [far_shape((S, F), BF), far_shape((S, F), BF), *halves, *halves, shape((1, F), F32),
         shape((1, D), F32), shape((1, D), F32)],
        (mod_in2, cotangent, mod, bias_up, pack_all),
        scratch=[pltpu.VMEM((F, D), BF), pltpu.VMEM((D, F), BF)],
        scalar=scalar, flops=8 * S * D * F, nbytes=12 * S * D,
    )
    def mlp_grads(after):
        late, _ = lax.optimization_barrier((dpre, after))
        return call(
            mlp_grad_body, (G,),
            [pl.BlockSpec((S, share), lambda i: (0, i)), full((S, F)), full((S, F)),
             pl.BlockSpec((S, share), lambda i: (0, i)), pl.BlockSpec((6, share), lambda i: (0, i))],
            pl.BlockSpec((1, 2 * F, share), lambda i: (i, 0, 0)), far_shape((G, 2 * F, share), BF),
            (mod_in2, late, activ, cotangent, mod), flops=4 * S * D * F, nbytes=8 * S * D,
        )

    din2, mlp_grad = fold(keep, send, T, mlp_grads)
    mlp_grad = lax.psum_scatter(mlp_grad.reshape(G * 2 * F, share), "dp", scatter_dimension=0, tiled=True)
    cot_rows = lax.dynamic_slice_in_dim(cotangent, t * rows, rows, 0)
    x_rows = lax.dynamic_slice_in_dim(inputs, t * rows, rows, 0)
    half = [full((1, rows, D // 2))] * 4
    own = full((rows, D))
    dres1, dbranch1, resid1, sums_mid = call(
        between_body, (1,), half + [own, full((6, D)), own, own], [own, own, own, full((3, D))],
        [shape((rows, D), F32), shape((rows, D), BF), shape((rows, D), F32), shape((3, D), F32)],
        (*din2, x_rows, mod, cot_rows, branch1), nbytes=24 * rows * D, near=True,
    )
    dbr_rel = spread(dbranch1, T)
    dqkv, qkv_sum, proj_sum, proj_grad = call(
        functools.partial(attend_back_body, T, rows), steps,
        [own] * T + [full((hc, D)), full((S, 3 * hc)), pl.BlockSpec((heads, blk), lambda i, *_: (0, i)),
                                         full((S, hc))],
        [full((S, 3 * hc)), full((1, 3 * hc)), full((1, D)), full((D, hc))],
        [shape((S, 3 * hc), BF), shape((1, 3 * hc), F32), shape((1, D), F32), shape((D, hc), BF)],
        (*dbr_rel, proj_own, qkv, lse, attended),
        scratch=[pltpu.VMEM((S, hc), BF), pltpu.VMEM((3 * heads, S, HD), F32)],
        scalar=scalar, flops=40 * S * S * hc, nbytes=6 * S * D,
    )
    keep1, send1, sums_in = call(
        functools.partial(leave_body, rows), pairs,
        [rows_of(pair, 3 * hc), full((D, 3 * hc)), rows_of(pair, D)],
        [place_pair, place_pair, full((2, D))],
        [*halves, shape((2, D), F32)],
        (dqkv, w_qkv_all, inputs), scalar=scalar, flops=6 * S * D * hc, nbytes=6 * S * D,
    )
    first_grad = call(
        first_grad_body, (G,),
        [pl.BlockSpec((S, share), lambda i, s_ref: (0, (i + s_ref[1]) % G)), full((S, 3 * hc)),
         pl.BlockSpec((share, hc), lambda i, s_ref: ((i + s_ref[1]) % G, 0))],
        pl.BlockSpec((1, share, 4 * hc), lambda i, *_: (i, 0, 0)), shape((G, share, 4 * hc), BF),
        (mod_in1, dqkv, proj_grad), scalar=scalar, flops=6 * S * D * hc, nbytes=4 * S * D,
    )

    sums_out = out_sum + bias_rows[1:2] * jnp.sum(cot_rows.astype(F32), 0, keepdims=True)
    dmod = jnp.concatenate([sums_in, sums_mid, sums_out], axis=0).reshape(T, ada)
    dmod = jnp.sum(lax.all_to_all(dmod, "tensor", 0, 0, tiled=True), 0)
    qkv_sum = qkv_sum.reshape(heads, 3, HD)
    message = jnp.concatenate(
        [dmod.astype(BF).astype(F32), qkv_sum[:, 0].reshape(-1), qkv_sum[:, 2].reshape(-1),
         up_sum.reshape(-1), proj_sum.reshape(-1), down_sum.reshape(-1)]
    ).reshape(1, -1)
    message_rel = jnp.concatenate(from_planes(message), axis=0)
    first_grad, message_rel, mlp_grad, keep1, keep2, send2 = lax.optimization_barrier(
        (first_grad, message_rel, mlp_grad, keep1, keep2, send2)
    )
    first_grads = [first_grad[0]] + [around(first_grad[k], k) for k in range(1, G)]
    din1 = fold(keep1, send1, T)
    input_grad = call(
        last_body, (1,), half + [own, full((6, D)), own], own, shape((rows, D), F32),
        (*din1, x_rows, mod, dres1), nbytes=14 * rows * D, near=True,
    )

    block_out = call(
        output_body, (1,), half + [full((1, D)), own, full((6, D))], own, shape((rows, D), F32),
        (*fold(keep2, send2, T), bias_rows[1:2], resid1, mod), nbytes=14 * rows * D, near=True,
    )
    dmod_rel = message_rel[:, :ada].astype(BF)
    bias_sum = jnp.sum(message_rel, 0)
    col_sum = lax.dynamic_slice_in_dim(bias_sum[: G * n_col], z * n_col, n_col, 0)
    row_sum = lax.dynamic_slice_in_dim(bias_sum[G * n_col :].reshape(2, D), z * share, share, 1)
    per = T // G
    grad_silu = dot(dmod_rel, ada_low, 1, 1).reshape(T, D // T)
    grad_silu = jnp.sum(lax.all_to_all(grad_silu, "tensor", 0, 0, tiled=True), 0, keepdims=True)
    grad_silu = lax.ppermute(
        grad_silu, ("dp", "tensor"),
        [(a * T + b, ((a - b // per) % G) * T + a * per + b % per) for a in range(G) for b in range(T)],
    )
    cond_here = lax.dynamic_slice_in_dim(cond, t * (D // T), D // T, 1)
    sig_here = jax.nn.sigmoid(cond_here)
    cond_grad = grad_silu * sig_here * (1.0 + cond_here * (1.0 - sig_here))

    wide = LR_SCALE * D ** (-0.5)
    chunk = ada // 3
    by_chunk = pl.BlockSpec((share, chunk), lambda i: (0, i))
    ada_out = call(
        functools.partial(adam_ada_body, wide), (3,),
        [full((G, share)), pl.BlockSpec((G, chunk), lambda i: (0, i))] + [by_chunk] * 3,
        [by_chunk] * 3, [far_shape((share, ada), F32)] * 3,
        (silu_own, dmod_rel, w_ada, m_ada, v_ada), nbytes=24 * share * ada,
    )
    wide_block, flat = full((share, 3 * hc)), full((hc, share))
    first_out = call(
        functools.partial(adam_first_body, G, wide, LR_SCALE * (D // 32) ** (-0.5)), (1,),
        [full((share, 4 * hc))] * G + [wide_block] * 3 + [flat] * 3, [wide_block] * 3 + [flat] * 3,
        [far_shape((share, 3 * hc), F32)] * 3 + [far_shape((hc, share), F32)] * 3,
        (*first_grads, w_qkv, m_qkv, v_qkv, w_proj, m_proj, v_proj), nbytes=32 * share * 4 * hc,
    )
    chunks = F // share
    square = (share, share)
    up_block = pl.BlockSpec(square, lambda i: (0, i))
    down_block = pl.BlockSpec(square, lambda i: (i, 0))
    mlp_out = call(
        functools.partial(adam_mlp_body, wide, LR_SCALE * (F * T) ** (-0.5)), (chunks,),
        [down_block, pl.BlockSpec(square, lambda i: (chunks + i, 0))] + [up_block] * 3 + [down_block] * 3,
        [up_block] * 3 + [down_block] * 3,
        [far_shape((share, F), F32)] * 3 + [far_shape((F, share), F32)] * 3,
        (mlp_grad, mlp_grad, w_fc1, m_fc1, v_fc1, w_fc2, m_fc2, v_fc2), nbytes=52 * share * F,
    )
    col_second, col_new = adam_step(col_bias, m_col, v_col, col_sum, LR_BIAS, 0.0)
    row_second, row_new = adam_step(row_bias, m_row, v_row, row_sum, LR_BIAS, 0.0)
    return (
        block_out, input_grad, cond_grad, *ada_out, *first_out, *mlp_out,
        col_sum, col_second, col_new, row_sum, row_second, row_new,
    )


def solution(mesh):
    by_cols = P("dp", "tensor")
    by_rows = P("tensor", "dp")
    column = P(("tensor", "dp"))
    row = P(None, "dp")
    tokens = P("dp", None)
    weights = (by_cols, by_cols, by_rows, by_cols, by_rows, column, row)
    moments = tuple(spec for spec in weights for _ in range(2))
    results = tuple(spec for spec in weights for _ in range(3))
    mine = P(("dp", "tensor"), None)
    return jax.shard_map(
        shards,
        mesh=mesh,
        in_specs=(tokens, tokens, tokens, *weights, *moments),
        out_specs=(mine, mine, by_cols, *results),
        check_vma=False,
    )
```

```python
import functools

import jax
import jax.numpy as jnp
from jax import lax
from jax.experimental import pallas as pl
from jax.experimental.pallas import tpu as pltpu
from jax.sharding import PartitionSpec as P

HD = 64
STEP = 10
LN_EPS = 1e-06
GELU_C = 0.7978845608028654
GELU_K = 0.044715
BETA_ONE = 0.9
BETA_TWO = 0.95
ADAM_EPS = 1e-08
DECAY = 0.1
LR_SCALE = 2.0
LR_BIAS = 0.2
BF = jnp.bfloat16
F32 = jnp.float32
MIB = 1024 * 1024


def dot(left, right, left_dim=1, right_dim=0):
    return lax.dot_general(
        left, right, (((left_dim,), (right_dim,)), ((), ())), preferred_element_type=F32
    )


def normalize(values):
    center = values - jnp.mean(values, -1, keepdims=True)
    inv_std = lax.rsqrt(jnp.mean(center * center, -1, keepdims=True) + LN_EPS)
    return (center * inv_std, inv_std)


def norm_back(grad_n, normed, inv_std):
    return inv_std * (
        grad_n
        - jnp.mean(grad_n, -1, keepdims=True)
        - normed * jnp.mean(grad_n * normed, -1, keepdims=True)
    )


def gelu_pair(values):
    square = values * values
    inner = GELU_C * (values + GELU_K * square * values)
    tanh_val = jnp.tanh(inner)
    half = 0.5 * (1.0 + tanh_val)
    result = values * half
    slope = half + 0.5 * values * (1.0 - tanh_val * tanh_val) * GELU_C * (
        1.0 + 3.0 * GELU_K * square
    )
    return (result, slope)


def full(shape):
    return pl.BlockSpec(shape, lambda *_: (0,) * len(shape))


def rows_of(count, width):
    return pl.BlockSpec((count, width), lambda i, *_: (i, 0))


def call(body, grid, in_specs, out_specs, out_shape, args, scratch=(), scalar=None, flops=0, nbytes=0, near=False, mib=56,
         far=()):
    params = pltpu.CompilerParams(vmem_limit_bytes=(16 if near else mib) * MIB)
    cost = pl.CostEstimate(flops=flops, bytes_accessed=nbytes, transcendentals=0)
    args = [
        pltpu.with_memory_space_constraint(a, pltpu.HBM) if n in far
        else pltpu.with_memory_space_constraint(a, pltpu.VMEM) if near else a
        for n, a in enumerate(args)
    ]
    if scalar is None:
        return pl.pallas_call(
            body, grid=grid, in_specs=in_specs, out_specs=out_specs, out_shape=out_shape,
            scratch_shapes=list(scratch), compiler_params=params, cost_estimate=cost,
        )(*args)
    spec = pltpu.PrefetchScalarGridSpec(
        num_scalar_prefetch=1, grid=grid, in_specs=in_specs, out_specs=out_specs,
        scratch_shapes=list(scratch),
    )
    return pl.pallas_call(
        body, grid_spec=spec, out_shape=out_shape, compiler_params=params, cost_estimate=cost,
    )(scalar, *args)


def far_shape(dims, dtype):
    return pltpu.HBM(dims, dtype)


def shape(dims, dtype):
    return jax.ShapeDtypeStruct(dims, dtype)


def mod_body(count, s_ref, *refs):
    small = refs[:count]
    w_ref, part_ref, silu_ref, low_ref = refs[count:]
    share = w_ref.shape[0]
    at = pl.ds(pl.multiple_of(s_ref[1] * share, share), share)
    low = w_ref[...].astype(BF)
    silu = jnp.concatenate([r[:, at] for r in small], axis=0).astype(BF)
    low_ref[...] = low
    silu_ref[...] = silu
    part_ref[...] = dot(silu, low)


def pack_first_body(qkv_ref, proj_ref, out_ref):
    width = qkv_ref.shape[1]
    out_ref[:, :width] = qkv_ref[...].astype(BF)
    out_ref[:, width:] = proj_ref[...].T.astype(BF)


def pack_body(up_ref, down_ref, out_ref):
    share, hidden = up_ref.shape
    for n in range(hidden // share):
        out_ref[n * share : (n + 1) * share, :] = up_ref[:, n * share : (n + 1) * share].astype(BF)
    out_ref[hidden:, :] = down_ref[...].astype(BF)


def unpack_first_body(first_ref, w_ref, proj_ref):
    width = w_ref.shape[1]
    w_ref[...] = first_ref[:, :width]
    proj_ref[...] = first_ref[:, width:].T


def enter_body(x_ref, mod_ref, bias_ref, w_ref, min_ref, qkv_ref):
    normed, _ = normalize(x_ref[...].astype(F32))
    low = (normed * (1.0 + mod_ref[1:2, :]) + mod_ref[0:1, :]).astype(BF)
    min_ref[...] = low
    qkv_ref[...] = (dot(low, w_ref[...]) + bias_ref[...]).astype(BF)


def attend_body(blk_ref, qkv_ref, out_ref, lse_ref):
    heads = lse_ref.shape[0]
    outs = []
    blk = blk_ref[...]
    allr = qkv_ref[...]
    for h in range(heads):
        base = h * 3 * HD
        query = blk[:, base : base + HD] * BF(HD ** (-0.5))
        key = allr[:, base + HD : base + 2 * HD]
        value = allr[:, base + 2 * HD : base + 3 * HD]
        scores = dot(key, query, 1, 1)
        highest = jnp.max(scores, 0, keepdims=True)
        expon = jnp.exp(scores - highest)
        totals = jnp.sum(expon, 0, keepdims=True)
        out = dot(value, expon.astype(BF), 0, 0) * (1.0 / totals)
        outs.append(out.T.astype(BF))
        lse_ref[h : h + 1, :] = highest + jnp.log(totals)
    out_ref[...] = outs[0] if heads == 1 else jnp.concatenate(outs, axis=1)


def middle_body(count, rows, s_ref, *refs):
    att = refs[:count]
    proj = refs[count : 2 * count]
    x_ref, mod_ref, bias_ref, min_ref, br_ref, proj_s, br_s = refs[2 * count :]
    block = x_ref.shape[0]
    step = pl.program_id(0)

    @pl.when(step == 0)
    def _():
        at = 0
        for ref in proj:
            proj_s[at : at + ref.shape[0], :] = ref[...]
            at += ref.shape[0]

    joined = jnp.concatenate([ref[...] for ref in att], axis=1)
    branch = dot(joined, proj_s[...]) + bias_ref[...]
    resid = x_ref[...].astype(F32) + mod_ref[2:3, :] * branch
    normed, _ = normalize(resid)
    min_ref[...] = (normed * (1.0 + mod_ref[4:5, :]) + mod_ref[3:4, :]).astype(BF)
    start = s_ref[0] * rows

    @pl.when(step == start // block)
    def _():
        br_s[...] = branch
        br_ref[...] = br_s[pl.ds(pl.multiple_of(start % block, rows), rows), :]


def store_pair(odd, value, rows, keep_ref, send_ref):
    low, high = value[:rows], value[rows:]
    keep_ref[0] = jnp.where(odd, high, low)
    send_ref[0] = jnp.where(odd, low, high)


def mlp_body(rows, s_ref, in_ref, cot_ref, mod_ref, bias_ref, pack_ref,
             act_ref, dpre_ref, keep_ref, send_ref, keep2_ref, send2_ref, upsum_ref, downsum_ref, outsum_ref,
             down_s, up_s):
    planes, _, share = pack_ref.shape
    hidden = act_ref.shape[1]

    @pl.when(pl.program_id(0) == 0)
    def _():
        for plane in range(planes):
            at = slice(plane * share, (plane + 1) * share)
            for n in range(hidden // share):
                up_s[at, n * share : (n + 1) * share] = pack_ref[plane, n * share : (n + 1) * share, :]
            down_s[:, at] = pack_ref[plane, hidden:, :]
        upsum_ref[...] = jnp.zeros_like(upsum_ref)
        downsum_ref[...] = jnp.zeros_like(downsum_ref)
        outsum_ref[...] = jnp.zeros_like(outsum_ref)

    up = up_s[...]
    down = down_s[...]
    odd = s_ref[0] % 2 == 1
    cot = cot_ref[...].astype(F32)
    pre = dot(in_ref[...], up) + bias_ref[...]
    act, slope = gelu_pair(pre)
    act = act.astype(BF)
    act_ref[...] = act
    grad_b = (cot * mod_ref[5:6, :]).astype(BF)
    dpre = (dot(grad_b, down, 1, 1) * slope).astype(BF)
    dpre_ref[...] = dpre
    store_pair(odd, dot(dpre, up, 1, 1).astype(BF), rows, keep_ref, send_ref)
    part = dot(act, down)
    store_pair(odd, part.astype(BF), rows, keep2_ref, send2_ref)
    outsum_ref[...] += jnp.sum(cot * part, 0, keepdims=True)
    upsum_ref[...] += jnp.sum(dpre.astype(F32), 0, keepdims=True)
    downsum_ref[...] += jnp.sum(grad_b.astype(F32), 0, keepdims=True)


def mlp_grad_body(in_ref, dpre_ref, act_ref, cot_ref, mod_ref, out_ref):
    hidden = act_ref.shape[1]
    share = in_ref.shape[1]
    up = dot(in_ref[...], dpre_ref[...], 0, 0).astype(BF)
    for n in range(hidden // share):
        out_ref[0, n * share : (n + 1) * share, :] = up[:, n * share : (n + 1) * share]
    grad_b = (cot_ref[...].astype(F32) * mod_ref[5:6, :]).astype(BF)
    out_ref[0, hidden:, :] = dot(act_ref[...], grad_b, 0, 0).astype(BF)


def first_grad_body(in_ref, dqkv_ref, proj_ref, out_ref):
    width = dqkv_ref.shape[1]
    out_ref[:, :width] = dot(in_ref[...], dqkv_ref[...], 0, 0).astype(BF)
    out_ref[:, width:] = proj_ref[...]


def split_left(total, keep_ref, send_ref, cols=slice(None)):
    for n in range(keep_ref.shape[0]):
        keep_ref[n, :, cols] = total[2 * n]
        send_ref[n, :, cols] = total[2 * n + 1].astype(BF)


def split_right(total, keep_ref, send_ref, cols=slice(None)):
    count = keep_ref.shape[0]
    for n in range(count):
        keep_ref[n, :, cols] = total[n]
        send_ref[n, :, cols] = total[count + n].astype(BF)


def fold_first_body(count, *refs):
    lk_ref, ls_ref, rk_ref, rs_ref = refs[2 * count :]
    half = refs[0].shape[2] // 2
    for n in range(count):
        total = refs[n][...].astype(F32) + refs[count + n][...].astype(F32)
        cols = slice(n * half, (n + 1) * half)
        split_left(total[:, :, :half], lk_ref, ls_ref, cols)
        split_right(total[:, :, half:], rk_ref, rs_ref, cols)


def fold_next_body(left_ref, lgot_ref, right_ref, rgot_ref, lk_ref, ls_ref, rk_ref, rs_ref):
    split_left(left_ref[...] + lgot_ref[...].astype(F32), lk_ref, ls_ref)
    split_right(right_ref[...] + rgot_ref[...].astype(F32), rk_ref, rs_ref)


def fold_last(refs, n=0, count=1):
    left, lgot, right, rgot = refs
    half = left.shape[2] // count
    cols = slice(n * half, (n + 1) * half)
    return jnp.concatenate(
        [left[0, :, cols] + lgot[0, :, cols].astype(F32), right[0, :, cols] + rgot[0, :, cols].astype(F32)], axis=1
    )


def between_body(*refs):
    x_ref, mod_ref, cot_ref, br_ref, dres_ref, dbr_ref, res_ref, sums_ref = refs[4:]
    din = fold_last(refs[:4])
    resid = x_ref[...].astype(F32) + mod_ref[2:3, :] * br_ref[...]
    res_ref[...] = resid
    normed, inv = normalize(resid)
    dres = cot_ref[...].astype(F32) + norm_back(din * (1.0 + mod_ref[4:5, :]), normed, inv)
    dres_ref[...] = dres
    dbr_ref[...] = (mod_ref[2:3, :] * dres).astype(BF)
    sums_ref[0:1, :] = jnp.sum(dres * br_ref[...], 0, keepdims=True)
    sums_ref[1:2, :] = jnp.sum(din, 0, keepdims=True)
    sums_ref[2:3, :] = jnp.sum(din * normed, 0, keepdims=True)


def attend_back_body(count, rows, s_ref, *refs):
    dbr = refs[:count]
    (proj_ref, qkv_ref, lse_ref, att_ref, out_ref, colsum_ref, projsum_ref, projgrad_ref,
     datt, acc) = refs[count:]
    heads = lse_ref.shape[0]
    seq = qkv_ref.shape[0]
    block = lse_ref.shape[1]
    step = pl.program_id(0)

    @pl.when(step == 0)
    def _():
        total = jnp.zeros(projsum_ref.shape, F32)
        grad = jnp.zeros(projgrad_ref.shape, F32)
        for r in range(count):
            block_in = dbr[r][...]
            at = pl.ds(pl.multiple_of((s_ref[0] ^ r) * rows, rows), rows)
            datt[at, :] = dot(block_in, proj_ref[...], 1, 1).astype(BF)
            total += jnp.sum(block_in.astype(F32), 0, keepdims=True)
            grad += dot(block_in, att_ref[at, :], 0, 0)
        projgrad_ref[...] = grad.astype(BF)
        projsum_ref[...] = total
        acc[...] = jnp.zeros_like(acc)

    here = pl.ds(pl.multiple_of(step * block, block), block)
    blk = qkv_ref[here, :]
    allr = qkv_ref[...]
    grads = datt[here, :]
    for h in range(heads):
        base = h * 3 * HD
        query = blk[:, base : base + HD] * BF(HD ** (-0.5))
        key = allr[:, base + HD : base + 2 * HD]
        value = allr[:, base + 2 * HD : base + 3 * HD]
        grad = grads[:, h * HD : (h + 1) * HD]
        prob = jnp.exp(dot(key, query, 1, 1) - lse_ref[h : h + 1, :])
        dprob = dot(value, grad, 1, 1)
        weighted = jnp.sum(prob * dprob, 0, keepdims=True)
        dscore = (prob * (dprob - weighted)).astype(BF)
        acc[3 * h, here, :] = dot(key, dscore, 0, 0).T * HD ** (-0.5)
        acc[3 * h + 1] += dot(dscore, query)
        acc[3 * h + 2] += dot(prob.astype(BF), grad)

    @pl.when(step == seq // block - 1)
    def _():
        result = jnp.concatenate([acc[n] for n in range(3 * heads)], axis=1).astype(BF)
        out_ref[...] = result
        colsum_ref[...] = jnp.sum(result.astype(F32), 0, keepdims=True)


def leave_body(rows, s_ref, dqkv_ref, w_ref, x_ref, keep_ref, send_ref, sums_ref):
    part = dot(dqkv_ref[...], w_ref[...], 1, 1)
    store_pair(s_ref[0] % 2 == 1, part.astype(BF), rows, keep_ref, send_ref)
    normed, _ = normalize(x_ref[...].astype(F32))

    @pl.when(pl.program_id(0) == 0)
    def _():
        sums_ref[...] = jnp.zeros_like(sums_ref)

    sums_ref[0:1, :] += jnp.sum(part, 0, keepdims=True)
    sums_ref[1:2, :] += jnp.sum(part * normed, 0, keepdims=True)


def finish_body(*refs):
    x_ref, mod_ref, dres_ref, bias_ref, res_ref, grad_ref, out_ref = refs[4:]
    normed, inv = normalize(x_ref[...].astype(F32))
    din = fold_last(refs[:4], 0, 2)
    grad_ref[...] = dres_ref[...] + norm_back(din * (1.0 + mod_ref[1:2, :]), normed, inv)
    out_ref[...] = res_ref[...] + mod_ref[5:6, :] * (fold_last(refs[:4], 1, 2) + bias_ref[...])


def adam_step(weight, first, second, grad, rate, decay):
    first_new = BETA_ONE * first + (1.0 - BETA_ONE) * grad
    second_new = BETA_TWO * second + (1.0 - BETA_TWO) * grad * grad
    fix_one = 1.0 - BETA_ONE**STEP
    fix_two = 1.0 - BETA_TWO**STEP
    step_dir = first_new / fix_one / (jnp.sqrt(second_new / fix_two) + ADAM_EPS)
    return (second_new, weight - rate * (step_dir + decay * weight))


def adam_store(grad, w_ref, m_ref, v_ref, grad_ref, second_ref, new_ref, rate):
    grad_ref[...] = grad
    second, new = adam_step(w_ref[...], m_ref[...], v_ref[...], grad, rate, DECAY)
    second_ref[...] = second
    new_ref[...] = new


def adam_first_body(rate_qkv, rate_proj, grad_ref, *refs):
    args, outs = refs[:6], refs[6:]
    width = args[0].shape[1]
    grad = grad_ref[...].astype(F32)
    adam_store(grad[:, :width], *args[:3], *outs[:3], rate_qkv)
    adam_store(grad[:, width:].T, *args[3:], *outs[3:], rate_proj)


def adam_ada_body(rate, silu_ref, dmod_ref, *refs):
    adam_store(dot(silu_ref[...], dmod_ref[...], 0, 0), *refs, rate)


def adam_mlp_body(rate_up, rate_down, gup_ref, gdown_ref, *refs):
    adam_store(gup_ref[...].astype(F32), *refs[0:3], *refs[6:9], rate_up)
    adam_store(gdown_ref[...].astype(F32), *refs[3:6], *refs[9:12], rate_down)


def swap(value, mask, size):
    return lax.ppermute(value, "tensor", [(i, i ^ mask) for i in range(size)])


def spread_first(block, size):
    return swap(block, 2, size), swap(block, 4, size), swap(block, 1, size)


def spread_second(near, size):
    by_x, by_y, _ = near
    return swap(by_x, 4, size), swap(by_x, 1, size), swap(by_y, 1, size)


def spread_third(block, near, more, size):
    by_x, by_y, core = near
    diag, core_x, core_y = more
    return [block, core, by_x, core_x, by_y, core_y, diag, swap(diag, 1, size)]


def spread(block, size):
    if size == 8:
        near = spread_first(block, size)
        return spread_third(block, near, spread_second(near, size), size)
    have = {0: block}
    bit = 1
    while bit < size:
        for r in list(have):
            have[r ^ bit] = swap(have[r], bit, size)
        bit *= 2
    return [have[r] for r in range(size)]


def fold(keeps, sends, size, beside=None):
    gots = [swap(send, 1, size) for send in sends]
    count, rows, width = keeps[0].shape
    half = width // 2 * len(keeps)
    left = right = done = None
    stage = 0
    while count > 1:
        count //= 2
        dims = (count, rows, half)
        outs = [shape(dims, F32), shape(dims, BF)] * 2
        specs = [full(dims)] * 4
        if left is None:
            args, body, far = (*keeps, *gots), functools.partial(fold_first_body, len(keeps)), range(len(keeps))
        else:
            args, body, far = (left, lgot, right, rgot), fold_next_body, ()
        left, lsend, right, rsend = call(
            body, (1,), [full(a.shape) for a in args], specs, outs, args,
            nbytes=40 * count * rows * half, near=True, far=far,
        )
        lgot = swap(lsend, 2 << stage, size)
        rgot = swap(rsend, (size // 2) >> stage, size)
        if beside is not None and stage == 0:
            done = beside(left)
            left, lgot, right, rgot, done = lax.optimization_barrier((left, lgot, right, rgot, done))
        stage += 1
    return (left, lgot, right, rgot), done


def shards(
    inputs, conditioning, cotangent, w_ada, w_qkv, w_proj, w_fc1, w_fc2, col_bias, row_bias,
    m_ada, v_ada, m_qkv, v_qkv, m_proj, v_proj, m_fc1, v_fc1, m_fc2, v_fc2, m_col, v_col, m_row, v_row,
):
    T = lax.axis_size("tensor")
    G = lax.axis_size("dp")
    t = lax.axis_index("tensor")
    z = lax.axis_index("dp")
    S, D = inputs.shape
    rows = S // T
    hc = w_proj.shape[0]
    heads = hc // HD
    F = w_fc1.shape[1]
    ada = w_ada.shape[1]
    share = D // G
    scalar = jnp.stack([t, z]).astype(jnp.int32)
    n_col = col_bias.shape[0]

    def around(value, k):
        return lax.ppermute(value, "dp", [(i, (i + k) % G) for i in range(G)])

    def from_planes(value):
        return [value] + [around(value, k) for k in range(1, G)]

    first = call(
        pack_first_body, (1,), [full((share, 3 * hc)), full((hc, share))], full((share, 4 * hc)),
        shape((share, 4 * hc), BF), (w_qkv, w_proj), nbytes=24 * hc * share,
    )
    pack = call(
        pack_body, (1,), [full((share, F)), full((F, share))], full((2 * F, share)),
        shape((2 * F, share), BF), (w_fc1, w_fc2), nbytes=12 * F * share,
    )
    first_all = lax.all_gather(first, "dp", axis=0, tiled=True)
    pack_all = lax.all_gather(pack, "dp", axis=0, tiled=False)

    cond = conditioning.astype(F32)
    silu = (cond * jax.nn.sigmoid(cond)).astype(BF).astype(F32)
    small = jnp.concatenate(
        [silu, col_bias.astype(BF).astype(F32).reshape(1, -1), row_bias.astype(BF).astype(F32).reshape(1, -1)],
        axis=1,
    )
    small_rel = from_planes(small)
    part, silu_own, ada_low = call(
        functools.partial(mod_body, G), (1,),
        [full(small.shape)] * G + [full((share, ada))],
        [full((G, ada)), full((G, share)), full((share, ada))],
        [shape((G, ada), F32), shape((G, share), BF), shape((share, ada), BF)],
        (*small_rel, w_ada), scalar=scalar, nbytes=8 * share * ada, near=True,
    )
    bias_rev = jnp.concatenate(small_rel[::-1] * 2, axis=0)[:, D:]
    bias_abs = lax.dynamic_slice_in_dim(bias_rev, G - 1 - z, G, 0)
    cols = bias_abs[:, :n_col].reshape(-1)
    bias_rows = bias_abs[:, n_col:].reshape(G, 2, share).transpose(1, 0, 2).reshape(2, D)
    bias_up = cols[ada + 2 * hc :].reshape(1, F)
    bias_qkv = jnp.stack(
        [cols[ada : ada + hc].reshape(heads, HD), jnp.zeros((heads, HD), F32),
         cols[ada + hc : ada + 2 * hc].reshape(heads, HD)], axis=1,
    ).reshape(1, 3 * hc)
    mod_part = part[0:1] + cols[:ada].reshape(1, ada)
    for k in range(1, G):
        mod_part = mod_part + around(part[k : k + 1], G - k)
    mod = lax.all_gather(mod_part, "tensor", axis=1, tiled=True).reshape(6, D)

    first_all, mod = lax.optimization_barrier((first_all, mod))
    w_qkv_all, proj_own = call(
        unpack_first_body, (1,), [full((D, 4 * hc))],
        [full((D, 3 * hc)), full((hc, D))], [shape((D, 3 * hc), BF), shape((hc, D), BF)],
        (first_all,), nbytes=20 * hc * D,
    )

    blk = min(256, S)
    steps = (S // blk,)
    wide_blk = min(1024, S)
    wide_steps = (S // wide_blk,)
    mod_in1, qkv = call(
        enter_body, steps,
        [rows_of(blk, D), full((6, D)), full((1, 3 * hc)), full((D, 3 * hc))],
        [rows_of(blk, D), rows_of(blk, 3 * hc)],
        [far_shape((S, D), BF), shape((S, 3 * hc), BF)],
        (inputs, mod, bias_qkv, w_qkv_all), flops=2 * S * D * 3 * hc, nbytes=6 * S * D,
    )
    attended, lse = call(
        attend_body, wide_steps,
        [rows_of(wide_blk, 3 * hc), full((S, 3 * hc))],
        [rows_of(wide_blk, hc), pl.BlockSpec((heads, wide_blk), lambda i: (0, i))],
        [shape((S, hc), BF), shape((heads, S), F32)],
        (qkv, qkv), flops=16 * S * S * hc, nbytes=4 * S * hc, mib=32,
    )
    if T == 8:
        proj_near, _ = lax.optimization_barrier((spread_first(proj_own, T), qkv))
        proj_more, attended = lax.optimization_barrier((spread_second(proj_near, T), attended))
        proj_all = spread_third(proj_own, proj_near, proj_more, T)
    else:
        proj_all = spread(proj_own, T)
    att_rel = spread(attended, T)
    mod_in2, branch1 = call(
        functools.partial(middle_body, T, rows), steps,
        [rows_of(blk, hc)] * T + [full((hc, D))] * T + [rows_of(blk, D), full((6, D)), full((1, D))],
        [rows_of(blk, D), full((rows, D))],
        [far_shape((S, D), BF), shape((rows, D), F32)],
        (*att_rel, *proj_all, inputs, mod, bias_rows[0:1]),
        scratch=[pltpu.VMEM((T * hc, D), BF), pltpu.VMEM((blk, D), F32)],
        scalar=scalar, flops=2 * S * D * D, nbytes=8 * S * D,
    )

    pair = 2 * rows
    pairs = (T // 2,)
    place_pair = pl.BlockSpec((1, rows, D), lambda i, s_ref: (i ^ (s_ref[0] // 2), 0, 0))
    halves = [shape((T // 2, rows, D), BF)] * 2
    activ, dpre, keep, send, keep2, send2, up_sum, down_sum, out_sum = call(
        functools.partial(mlp_body, rows), pairs,
        [rows_of(pair, D), rows_of(pair, D), full((6, D)), full((1, F))]
        + [full((G, 2 * F, share))],
        [rows_of(pair, F), rows_of(pair, F)] + [place_pair] * 4 + [full((1, F)), full((1, D)), full((1, D))],
        [far_shape((S, F), BF), far_shape((S, F), BF), *halves, *halves, shape((1, F), F32),
         shape((1, D), F32), shape((1, D), F32)],
        (mod_in2, cotangent, mod, bias_up, pack_all),
        scratch=[pltpu.VMEM((F, D), BF), pltpu.VMEM((D, F), BF)],
        scalar=scalar, flops=8 * S * D * F, nbytes=12 * S * D,
    )
    def mlp_grads(after):
        late, _ = lax.optimization_barrier((dpre, after))
        return call(
            mlp_grad_body, (G,),
            [pl.BlockSpec((S, share), lambda i: (0, i)), full((S, F)), full((S, F)),
             pl.BlockSpec((S, share), lambda i: (0, i)), pl.BlockSpec((6, share), lambda i: (0, i))],
            pl.BlockSpec((1, 2 * F, share), lambda i: (i, 0, 0)), far_shape((G, 2 * F, share), BF),
            (mod_in2, late, activ, cotangent, mod), flops=4 * S * D * F, nbytes=8 * S * D,
        )

    din2, mlp_grad = fold([keep], [send], T, mlp_grads)
    mlp_grad = lax.psum_scatter(mlp_grad.reshape(G * 2 * F, share), "dp", scatter_dimension=0, tiled=True)
    cot_rows = lax.dynamic_slice_in_dim(cotangent, t * rows, rows, 0)
    x_rows = lax.dynamic_slice_in_dim(inputs, t * rows, rows, 0)
    half = [full((1, rows, D // 2))] * 4
    own = full((rows, D))
    dres1, dbranch1, resid1, sums_mid = call(
        between_body, (1,), half + [own, full((6, D)), own, own], [own, own, own, full((3, D))],
        [far_shape((rows, D), F32), shape((rows, D), BF), far_shape((rows, D), F32), shape((3, D), F32)],
        (*din2, x_rows, mod, cot_rows, branch1), nbytes=24 * rows * D, near=True,
    )
    dbr_rel = spread(dbranch1, T)
    dqkv, qkv_sum, proj_sum, proj_grad = call(
        functools.partial(attend_back_body, T, rows), wide_steps,
        [own] * T + [full((hc, D)), full((S, 3 * hc)), pl.BlockSpec((heads, wide_blk), lambda i, *_: (0, i)),
                                         full((S, hc))],
        [full((S, 3 * hc)), full((1, 3 * hc)), full((1, D)), full((D, hc))],
        [shape((S, 3 * hc), BF), shape((1, 3 * hc), F32), shape((1, D), F32), shape((D, hc), BF)],
        (*dbr_rel, proj_own, qkv, lse, attended),
        scratch=[pltpu.VMEM((S, hc), BF), pltpu.VMEM((3 * heads, S, HD), F32)],
        scalar=scalar, flops=40 * S * S * hc, nbytes=6 * S * D,
    )
    keep1, send1, sums_in = call(
        functools.partial(leave_body, rows), pairs,
        [rows_of(pair, 3 * hc), full((D, 3 * hc)), rows_of(pair, D)],
        [place_pair, place_pair, full((2, D))],
        [far_shape((T // 2, rows, D), BF)] * 2 + [shape((2, D), F32)],
        (dqkv, w_qkv_all, inputs), scalar=scalar, flops=6 * S * D * hc, nbytes=6 * S * D, mib=32, far=(2,),
    )
    sums_out = out_sum + bias_rows[1:2] * jnp.sum(cot_rows.astype(F32), 0, keepdims=True)
    dmod = jnp.concatenate([sums_in, sums_mid, sums_out], axis=0).reshape(T, ada)
    dmod, mlp_grad, keep2, send2 = lax.optimization_barrier((dmod, mlp_grad, keep2, send2))
    dmod = jnp.sum(lax.all_to_all(dmod, "tensor", 0, 0, tiled=True), 0)
    dqkv_late, dmod = lax.optimization_barrier((dqkv, dmod))
    first_grad = call(
        first_grad_body, (G,),
        [pl.BlockSpec((S, share), lambda i: (0, i)), full((S, 3 * hc)), pl.BlockSpec((share, hc), lambda i: (i, 0))],
        pl.BlockSpec((share, 4 * hc), lambda i: (i, 0)), far_shape((D, 4 * hc), BF),
        (mod_in1, dqkv_late, proj_grad), flops=6 * S * D * hc, nbytes=4 * S * D, mib=32, far=(0,),
    )
    first_grad = lax.psum_scatter(first_grad, "dp", scatter_dimension=0, tiled=True)
    qkv_sum = qkv_sum.reshape(heads, 3, HD)
    message = jnp.concatenate(
        [dmod.astype(BF).astype(F32), qkv_sum[:, 0].reshape(-1), qkv_sum[:, 2].reshape(-1),
         up_sum.reshape(-1), proj_sum.reshape(-1), down_sum.reshape(-1)]
    ).reshape(1, -1)
    message_rel = jnp.concatenate(from_planes(message), axis=0)
    keep1, message_rel = lax.optimization_barrier((keep1, message_rel))
    sums, _ = fold([keep1, keep2], [send1, send2], T)
    input_grad, block_out = call(
        finish_body, (1,), [full((1, rows, D))] * 4 + [own, full((6, D)), own, full((1, D)), own], [own, own],
        [far_shape((rows, D), F32)] * 2,
        (*sums, x_rows, mod, dres1, bias_rows[1:2], resid1), nbytes=28 * rows * D, near=True, far=(6, 8),
    )
    dmod_rel = message_rel[:, :ada].astype(BF)
    bias_sum = jnp.sum(message_rel, 0)
    col_sum = lax.dynamic_slice_in_dim(bias_sum[: G * n_col], z * n_col, n_col, 0)
    row_sum = lax.dynamic_slice_in_dim(bias_sum[G * n_col :].reshape(2, D), z * share, share, 1)
    per = T // G
    grad_silu = dot(dmod_rel, ada_low, 1, 1).reshape(T, D // T)
    grad_silu = jnp.sum(lax.all_to_all(grad_silu, "tensor", 0, 0, tiled=True), 0, keepdims=True)
    grad_silu = lax.ppermute(
        grad_silu, ("dp", "tensor"),
        [(a * T + b, ((a - b // per) % G) * T + a * per + b % per) for a in range(G) for b in range(T)],
    )
    cond_here = lax.dynamic_slice_in_dim(cond, t * (D // T), D // T, 1)
    sig_here = jax.nn.sigmoid(cond_here)
    cond_grad = grad_silu * sig_here * (1.0 + cond_here * (1.0 - sig_here))

    wide = LR_SCALE * D ** (-0.5)
    chunk = ada // 3
    by_chunk = pl.BlockSpec((share, chunk), lambda i: (0, i))
    ada_out = call(
        functools.partial(adam_ada_body, wide), (3,),
        [full((G, share)), pl.BlockSpec((G, chunk), lambda i: (0, i))] + [by_chunk] * 3,
        [by_chunk] * 3, [far_shape((share, ada), F32)] * 3,
        (silu_own, dmod_rel, w_ada, m_ada, v_ada), nbytes=24 * share * ada,
    )
    wide_block, flat = full((share, 3 * hc)), full((hc, share))
    first_out = call(
        functools.partial(adam_first_body, wide, LR_SCALE * (D // 32) ** (-0.5)), (1,),
        [full((share, 4 * hc))] + [wide_block] * 3 + [flat] * 3, [wide_block] * 3 + [flat] * 3,
        [far_shape((share, 3 * hc), F32)] * 3 + [far_shape((hc, share), F32)] * 3,
        (first_grad, w_qkv, m_qkv, v_qkv, w_proj, m_proj, v_proj), nbytes=32 * share * 4 * hc,
    )
    chunks = F // share
    square = (share, share)
    up_block = pl.BlockSpec(square, lambda i: (0, i))
    down_block = pl.BlockSpec(square, lambda i: (i, 0))
    mlp_out = call(
        functools.partial(adam_mlp_body, wide, LR_SCALE * (F * T) ** (-0.5)), (chunks,),
        [down_block, pl.BlockSpec(square, lambda i: (chunks + i, 0))] + [up_block] * 3 + [down_block] * 3,
        [up_block] * 3 + [down_block] * 3,
        [far_shape((share, F), F32)] * 3 + [far_shape((F, share), F32)] * 3,
        (mlp_grad, mlp_grad, w_fc1, m_fc1, v_fc1, w_fc2, m_fc2, v_fc2), nbytes=52 * share * F,
    )
    col_second, col_new = adam_step(col_bias, m_col, v_col, col_sum, LR_BIAS, 0.0)
    row_second, row_new = adam_step(row_bias, m_row, v_row, row_sum, LR_BIAS, 0.0)
    return (
        block_out, input_grad, cond_grad, *ada_out, *first_out, *mlp_out,
        col_sum, col_second, col_new, row_sum, row_second, row_new,
    )


def solution(mesh):
    by_cols = P("dp", "tensor")
    by_rows = P("tensor", "dp")
    column = P(("tensor", "dp"))
    row = P(None, "dp")
    tokens = P("dp", None)
    weights = (by_cols, by_cols, by_rows, by_cols, by_rows, column, row)
    moments = tuple(spec for spec in weights for _ in range(2))
    results = tuple(spec for spec in weights for _ in range(3))
    mine = P(("dp", "tensor"), None)
    return jax.shard_map(
        shards,
        mesh=mesh,
        in_specs=(tokens, tokens, tokens, *weights, *moments),
        out_specs=(mine, mine, by_cols, *results),
        check_vma=False,
    )
```

```python
import functools

import jax
import jax.numpy as jnp
from jax import lax
from jax.experimental import pallas as pl
from jax.experimental.pallas import tpu as pltpu
from jax.sharding import PartitionSpec as P

HD = 64
STEP = 10
LN_EPS = 1e-06
GELU_C = 0.7978845608028654
GELU_K = 0.044715
BETA_ONE = 0.9
BETA_TWO = 0.95
ADAM_EPS = 1e-08
DECAY = 0.1
LR_SCALE = 2.0
LR_BIAS = 0.2
BF = jnp.bfloat16
F32 = jnp.float32
MIB = 1024 * 1024


def dot(left, right, left_dim=1, right_dim=0):
    return lax.dot_general(
        left, right, (((left_dim,), (right_dim,)), ((), ())), preferred_element_type=F32
    )


def normalize(values):
    center = values - jnp.mean(values, -1, keepdims=True)
    inv_std = lax.rsqrt(jnp.mean(center * center, -1, keepdims=True) + LN_EPS)
    return (center * inv_std, inv_std)


def norm_back(grad_n, normed, inv_std):
    return inv_std * (
        grad_n
        - jnp.mean(grad_n, -1, keepdims=True)
        - normed * jnp.mean(grad_n * normed, -1, keepdims=True)
    )


def gelu_pair(values):
    square = values * values
    inner = GELU_C * (values + GELU_K * square * values)
    tanh_val = jnp.tanh(inner)
    half = 0.5 * (1.0 + tanh_val)
    result = values * half
    slope = half + 0.5 * values * (1.0 - tanh_val * tanh_val) * GELU_C * (
        1.0 + 3.0 * GELU_K * square
    )
    return (result, slope)


def full(shape):
    return pl.BlockSpec(shape, lambda *_: (0,) * len(shape))


def rows_of(count, width):
    return pl.BlockSpec((count, width), lambda i, *_: (i, 0))


def call(body, grid, in_specs, out_specs, out_shape, args, scratch=(), scalar=None, flops=0, nbytes=0, near=False, mib=56,
         far=()):
    params = pltpu.CompilerParams(vmem_limit_bytes=(16 if near else mib) * MIB)
    cost = pl.CostEstimate(flops=flops, bytes_accessed=nbytes, transcendentals=0)
    args = [
        pltpu.with_memory_space_constraint(a, pltpu.HBM) if n in far
        else pltpu.with_memory_space_constraint(a, pltpu.VMEM) if near else a
        for n, a in enumerate(args)
    ]
    if scalar is None:
        return pl.pallas_call(
            body, grid=grid, in_specs=in_specs, out_specs=out_specs, out_shape=out_shape,
            scratch_shapes=list(scratch), compiler_params=params, cost_estimate=cost,
        )(*args)
    spec = pltpu.PrefetchScalarGridSpec(
        num_scalar_prefetch=1, grid=grid, in_specs=in_specs, out_specs=out_specs,
        scratch_shapes=list(scratch),
    )
    return pl.pallas_call(
        body, grid_spec=spec, out_shape=out_shape, compiler_params=params, cost_estimate=cost,
    )(scalar, *args)


def far_shape(dims, dtype):
    return pltpu.HBM(dims, dtype)


def shape(dims, dtype):
    return jax.ShapeDtypeStruct(dims, dtype)


def mod_body(count, s_ref, *refs):
    small = refs[:count]
    w_ref, part_ref, silu_ref, low_ref = refs[count:]
    share = w_ref.shape[0]
    at = pl.ds(pl.multiple_of(s_ref[1] * share, share), share)
    low = w_ref[...].astype(BF)
    silu = jnp.concatenate([r[:, at] for r in small], axis=0).astype(BF)
    low_ref[...] = low
    silu_ref[...] = silu
    part_ref[...] = dot(silu, low)


def pack_first_body(qkv_ref, proj_ref, out_ref):
    width = qkv_ref.shape[1]
    out_ref[:, :width] = qkv_ref[...].astype(BF)
    out_ref[:, width:] = proj_ref[...].T.astype(BF)


def pack_body(up_ref, down_ref, out_ref):
    share, hidden = up_ref.shape
    for n in range(hidden // share):
        out_ref[n * share : (n + 1) * share, :] = up_ref[:, n * share : (n + 1) * share].astype(BF)
    out_ref[hidden:, :] = down_ref[...].astype(BF)


def unpack_first_body(first_ref, w_ref, proj_ref):
    width = w_ref.shape[1]
    w_ref[...] = first_ref[:, :width]
    proj_ref[...] = first_ref[:, width:].T


def enter_body(x_ref, mod_ref, bias_ref, w_ref, min_ref, qkv_ref):
    normed, _ = normalize(x_ref[...].astype(F32))
    low = (normed * (1.0 + mod_ref[1:2, :]) + mod_ref[0:1, :]).astype(BF)
    min_ref[...] = low
    qkv_ref[...] = (dot(low, w_ref[...]) + bias_ref[...]).astype(BF)


def attend_body(blk_ref, qkv_ref, out_ref, lse_ref):
    heads = lse_ref.shape[0]
    outs = []
    blk = blk_ref[...]
    allr = qkv_ref[...]
    for h in range(heads):
        base = h * 3 * HD
        query = blk[:, base : base + HD] * BF(HD ** (-0.5))
        key = allr[:, base + HD : base + 2 * HD]
        value = allr[:, base + 2 * HD : base + 3 * HD]
        scores = dot(key, query, 1, 1)
        highest = jnp.max(scores, 0, keepdims=True)
        expon = jnp.exp(scores - highest)
        totals = jnp.sum(expon, 0, keepdims=True)
        out = dot(value, expon.astype(BF), 0, 0) * (1.0 / totals)
        outs.append(out.T.astype(BF))
        lse_ref[h : h + 1, :] = highest + jnp.log(totals)
    out_ref[...] = outs[0] if heads == 1 else jnp.concatenate(outs, axis=1)


def middle_body(count, rows, s_ref, *refs):
    att = refs[:count]
    proj = refs[count : 2 * count]
    x_ref, mod_ref, bias_ref, min_ref, br_ref, proj_s, br_s = refs[2 * count :]
    block = x_ref.shape[0]
    step = pl.program_id(0)

    @pl.when(step == 0)
    def _():
        at = 0
        for ref in proj:
            proj_s[at : at + ref.shape[0], :] = ref[...]
            at += ref.shape[0]

    joined = jnp.concatenate([ref[...] for ref in att], axis=1)
    branch = dot(joined, proj_s[...]) + bias_ref[...]
    resid = x_ref[...].astype(F32) + mod_ref[2:3, :] * branch
    normed, _ = normalize(resid)
    min_ref[...] = (normed * (1.0 + mod_ref[4:5, :]) + mod_ref[3:4, :]).astype(BF)
    start = s_ref[0] * rows

    @pl.when(step == start // block)
    def _():
        br_s[...] = branch
        br_ref[...] = br_s[pl.ds(pl.multiple_of(start % block, rows), rows), :]


def store_pair(odd, value, rows, keep_ref, send_ref):
    low, high = value[:rows], value[rows:]
    keep_ref[0] = jnp.where(odd, high, low)
    send_ref[0] = jnp.where(odd, low, high)


def mlp_body(rows, s_ref, in_ref, cot_ref, mod_ref, bias_ref, pack_ref,
             act_ref, dpre_ref, keep_ref, send_ref, keep2_ref, send2_ref, upsum_ref, downsum_ref, outsum_ref,
             down_s, up_s):
    planes, _, share = pack_ref.shape
    hidden = act_ref.shape[1]

    @pl.when(pl.program_id(0) == 0)
    def _():
        for plane in range(planes):
            at = slice(plane * share, (plane + 1) * share)
            for n in range(hidden // share):
                up_s[at, n * share : (n + 1) * share] = pack_ref[plane, n * share : (n + 1) * share, :]
            down_s[:, at] = pack_ref[plane, hidden:, :]
        upsum_ref[...] = jnp.zeros_like(upsum_ref)
        downsum_ref[...] = jnp.zeros_like(downsum_ref)
        outsum_ref[...] = jnp.zeros_like(outsum_ref)

    up = up_s[...]
    down = down_s[...]
    odd = s_ref[0] % 2 == 1
    cot = cot_ref[...].astype(F32)
    pre = dot(in_ref[...], up) + bias_ref[...]
    act, slope = gelu_pair(pre)
    act = act.astype(BF)
    act_ref[...] = act
    grad_b = (cot * mod_ref[5:6, :]).astype(BF)
    dpre = (dot(grad_b, down, 1, 1) * slope).astype(BF)
    dpre_ref[...] = dpre
    store_pair(odd, dot(dpre, up, 1, 1).astype(BF), rows, keep_ref, send_ref)
    part = dot(act, down)
    store_pair(odd, part.astype(BF), rows, keep2_ref, send2_ref)
    outsum_ref[...] += jnp.sum(cot * part, 0, keepdims=True)
    upsum_ref[...] += jnp.sum(dpre.astype(F32), 0, keepdims=True)
    downsum_ref[...] += jnp.sum(grad_b.astype(F32), 0, keepdims=True)


def mlp_grad_body(in_ref, dpre_ref, act_ref, cot_ref, mod_ref, out_ref):
    hidden = act_ref.shape[1]
    share = in_ref.shape[1]
    up = dot(in_ref[...], dpre_ref[...], 0, 0).astype(BF)
    for n in range(hidden // share):
        out_ref[0, n * share : (n + 1) * share, :] = up[:, n * share : (n + 1) * share]
    grad_b = (cot_ref[...].astype(F32) * mod_ref[5:6, :]).astype(BF)
    out_ref[0, hidden:, :] = dot(act_ref[...], grad_b, 0, 0).astype(BF)


def first_grad_body(in_ref, dqkv_ref, proj_ref, out_ref):
    width = dqkv_ref.shape[1]
    out_ref[:, :width] = dot(in_ref[...], dqkv_ref[...], 0, 0).astype(BF)
    out_ref[:, width:] = proj_ref[...]


def split_left(total, keep_ref, send_ref, cols=slice(None)):
    for n in range(keep_ref.shape[0]):
        keep_ref[n, :, cols] = total[2 * n]
        send_ref[n, :, cols] = total[2 * n + 1].astype(BF)


def split_right(total, keep_ref, send_ref, cols=slice(None)):
    count = keep_ref.shape[0]
    for n in range(count):
        keep_ref[n, :, cols] = total[n]
        send_ref[n, :, cols] = total[count + n].astype(BF)


def fold_first_body(count, *refs):
    lk_ref, ls_ref, rk_ref, rs_ref = refs[2 * count :]
    half = refs[0].shape[2] // 2
    for n in range(count):
        total = refs[n][...].astype(F32) + refs[count + n][...].astype(F32)
        cols = slice(n * half, (n + 1) * half)
        split_left(total[:, :, :half], lk_ref, ls_ref, cols)
        split_right(total[:, :, half:], rk_ref, rs_ref, cols)


def fold_next_body(left_ref, lgot_ref, right_ref, rgot_ref, lk_ref, ls_ref, rk_ref, rs_ref):
    split_left(left_ref[...] + lgot_ref[...].astype(F32), lk_ref, ls_ref)
    split_right(right_ref[...] + rgot_ref[...].astype(F32), rk_ref, rs_ref)


def fold_last(refs, n=0, count=1):
    left, lgot, right, rgot = refs
    half = left.shape[2] // count
    cols = slice(n * half, (n + 1) * half)
    return jnp.concatenate(
        [left[0, :, cols] + lgot[0, :, cols].astype(F32), right[0, :, cols] + rgot[0, :, cols].astype(F32)], axis=1
    )


def between_body(*refs):
    x_ref, mod_ref, cot_ref, br_ref, dres_ref, dbr_ref, res_ref, sums_ref = refs[4:]
    din = fold_last(refs[:4])
    resid = x_ref[...].astype(F32) + mod_ref[2:3, :] * br_ref[...]
    res_ref[...] = resid
    normed, inv = normalize(resid)
    dres = cot_ref[...].astype(F32) + norm_back(din * (1.0 + mod_ref[4:5, :]), normed, inv)
    dres_ref[...] = dres
    dbr_ref[...] = (mod_ref[2:3, :] * dres).astype(BF)
    sums_ref[0:1, :] = jnp.sum(dres * br_ref[...], 0, keepdims=True)
    sums_ref[1:2, :] = jnp.sum(din, 0, keepdims=True)
    sums_ref[2:3, :] = jnp.sum(din * normed, 0, keepdims=True)


def attend_back_body(count, rows, s_ref, *refs):
    dbr = refs[:count]
    (proj_ref, qkv_ref, lse_ref, att_ref, out_ref, colsum_ref, projsum_ref, projgrad_ref,
     datt, acc) = refs[count:]
    heads = lse_ref.shape[0]
    seq = qkv_ref.shape[0]
    block = lse_ref.shape[1]
    step = pl.program_id(0)

    @pl.when(step == 0)
    def _():
        total = jnp.zeros(projsum_ref.shape, F32)
        grad = jnp.zeros(projgrad_ref.shape, F32)
        for r in range(count):
            block_in = dbr[r][...]
            at = pl.ds(pl.multiple_of((s_ref[0] ^ r) * rows, rows), rows)
            datt[at, :] = dot(block_in, proj_ref[...], 1, 1).astype(BF)
            total += jnp.sum(block_in.astype(F32), 0, keepdims=True)
            grad += dot(block_in, att_ref[at, :], 0, 0)
        projgrad_ref[...] = grad.astype(BF)
        projsum_ref[...] = total
        acc[...] = jnp.zeros_like(acc)

    here = pl.ds(pl.multiple_of(step * block, block), block)
    blk = qkv_ref[here, :]
    allr = qkv_ref[...]
    grads = datt[here, :]
    for h in range(heads):
        base = h * 3 * HD
        query = blk[:, base : base + HD] * BF(HD ** (-0.5))
        key = allr[:, base + HD : base + 2 * HD]
        value = allr[:, base + 2 * HD : base + 3 * HD]
        grad = grads[:, h * HD : (h + 1) * HD]
        prob = jnp.exp(dot(key, query, 1, 1) - lse_ref[h : h + 1, :])
        dprob = dot(value, grad, 1, 1)
        weighted = jnp.sum(prob * dprob, 0, keepdims=True)
        dscore = (prob * (dprob - weighted)).astype(BF)
        acc[3 * h, here, :] = dot(key, dscore, 0, 0).T * HD ** (-0.5)
        acc[3 * h + 1] += dot(dscore, query)
        acc[3 * h + 2] += dot(prob.astype(BF), grad)

    @pl.when(step == seq // block - 1)
    def _():
        result = jnp.concatenate([acc[n] for n in range(3 * heads)], axis=1).astype(BF)
        out_ref[...] = result
        colsum_ref[...] = jnp.sum(result.astype(F32), 0, keepdims=True)


def leave_body(rows, s_ref, dqkv_ref, w_ref, x_ref, keep_ref, send_ref, sums_ref):
    part = dot(dqkv_ref[...], w_ref[...], 1, 1)
    store_pair(s_ref[0] % 2 == 1, part.astype(BF), rows, keep_ref, send_ref)
    normed, _ = normalize(x_ref[...].astype(F32))

    @pl.when(pl.program_id(0) == 0)
    def _():
        sums_ref[...] = jnp.zeros_like(sums_ref)

    sums_ref[0:1, :] += jnp.sum(part, 0, keepdims=True)
    sums_ref[1:2, :] += jnp.sum(part * normed, 0, keepdims=True)


def finish_body(*refs):
    x_ref, mod_ref, dres_ref, bias_ref, res_ref, grad_ref, out_ref = refs[4:]
    normed, inv = normalize(x_ref[...].astype(F32))
    din = fold_last(refs[:4], 0, 2)
    grad_ref[...] = dres_ref[...] + norm_back(din * (1.0 + mod_ref[1:2, :]), normed, inv)
    out_ref[...] = res_ref[...] + mod_ref[5:6, :] * (fold_last(refs[:4], 1, 2) + bias_ref[...])


def adam_step(weight, first, second, grad, rate, decay):
    first_new = BETA_ONE * first + (1.0 - BETA_ONE) * grad
    second_new = BETA_TWO * second + (1.0 - BETA_TWO) * grad * grad
    fix_one = 1.0 - BETA_ONE**STEP
    fix_two = 1.0 - BETA_TWO**STEP
    step_dir = first_new / fix_one / (jnp.sqrt(second_new / fix_two) + ADAM_EPS)
    return (second_new, weight - rate * (step_dir + decay * weight))


def adam_store(grad, w_ref, m_ref, v_ref, grad_ref, second_ref, new_ref, rate):
    grad_ref[...] = grad
    second, new = adam_step(w_ref[...], m_ref[...], v_ref[...], grad, rate, DECAY)
    second_ref[...] = second
    new_ref[...] = new


def adam_first_body(rate_qkv, rate_proj, grad_ref, *refs):
    args, outs = refs[:6], refs[6:]
    width = args[0].shape[1]
    grad = grad_ref[...].astype(F32)
    adam_store(grad[:, :width], *args[:3], *outs[:3], rate_qkv)
    adam_store(grad[:, width:].T, *args[3:], *outs[3:], rate_proj)


def adam_ada_body(rate, silu_ref, dmod_ref, *refs):
    adam_store(dot(silu_ref[...], dmod_ref[...], 0, 0), *refs, rate)


def adam_mlp_body(rate_up, rate_down, gup_ref, gdown_ref, *refs):
    adam_store(gup_ref[...].astype(F32), *refs[0:3], *refs[6:9], rate_up)
    adam_store(gdown_ref[...].astype(F32), *refs[3:6], *refs[9:12], rate_down)


def swap(value, mask, size):
    return lax.ppermute(value, "tensor", [(i, i ^ mask) for i in range(size)])


def spread_first(block, size):
    return swap(block, 2, size), swap(block, 4, size), swap(block, 1, size)


def spread_second(near, size):
    by_x, by_y, _ = near
    return swap(by_x, 4, size), swap(by_x, 1, size), swap(by_y, 1, size)


def spread_third(block, near, more, size):
    by_x, by_y, core = near
    diag, core_x, core_y = more
    return [block, core, by_x, core_x, by_y, core_y, diag, swap(diag, 1, size)]


def spread(block, size):
    if size == 8:
        near = spread_first(block, size)
        return spread_third(block, near, spread_second(near, size), size)
    have = {0: block}
    bit = 1
    while bit < size:
        for r in list(have):
            have[r ^ bit] = swap(have[r], bit, size)
        bit *= 2
    return [have[r] for r in range(size)]


def fold(keeps, sends, size, beside=None):
    gots = [swap(send, 1, size) for send in sends]
    count, rows, width = keeps[0].shape
    half = width // 2 * len(keeps)
    left = right = done = None
    stage = 0
    while count > 1:
        count //= 2
        dims = (count, rows, half)
        outs = [shape(dims, F32), shape(dims, BF)] * 2
        specs = [full(dims)] * 4
        if left is None:
            args, body, far = (*keeps, *gots), functools.partial(fold_first_body, len(keeps)), range(len(keeps) ** 2)
        else:
            args, body, far = (left, lgot, right, rgot), fold_next_body, ()
        left, lsend, right, rsend = call(
            body, (1,), [full(a.shape) for a in args], specs, outs, args,
            nbytes=40 * count * rows * half, near=True, far=far,
        )
        lgot = swap(lsend, 2 << stage, size)
        rgot = swap(rsend, (size // 2) >> stage, size)
        if beside is not None and stage == 0:
            done = beside(left)
            left, lgot, right, rgot, done = lax.optimization_barrier((left, lgot, right, rgot, done))
        stage += 1
    return (left, lgot, right, rgot), done


def shards(
    inputs, conditioning, cotangent, w_ada, w_qkv, w_proj, w_fc1, w_fc2, col_bias, row_bias,
    m_ada, v_ada, m_qkv, v_qkv, m_proj, v_proj, m_fc1, v_fc1, m_fc2, v_fc2, m_col, v_col, m_row, v_row,
):
    T = lax.axis_size("tensor")
    G = lax.axis_size("dp")
    t = lax.axis_index("tensor")
    z = lax.axis_index("dp")
    S, D = inputs.shape
    rows = S // T
    hc = w_proj.shape[0]
    heads = hc // HD
    F = w_fc1.shape[1]
    ada = w_ada.shape[1]
    share = D // G
    scalar = jnp.stack([t, z]).astype(jnp.int32)
    n_col = col_bias.shape[0]

    def around(value, k):
        return lax.ppermute(value, "dp", [(i, (i + k) % G) for i in range(G)])

    def from_planes(value):
        return [value] + [around(value, k) for k in range(1, G)]

    first = call(
        pack_first_body, (1,), [full((share, 3 * hc)), full((hc, share))], full((share, 4 * hc)),
        shape((share, 4 * hc), BF), (w_qkv, w_proj), nbytes=24 * hc * share,
    )
    pack = call(
        pack_body, (1,), [full((share, F)), full((F, share))], full((2 * F, share)),
        shape((2 * F, share), BF), (w_fc1, w_fc2), nbytes=12 * F * share,
    )
    first_all = lax.all_gather(first, "dp", axis=0, tiled=True)
    pack_all = lax.all_gather(pack, "dp", axis=0, tiled=False)

    cond = conditioning.astype(F32)
    silu = (cond * jax.nn.sigmoid(cond)).astype(BF).astype(F32)
    small = jnp.concatenate(
        [silu, col_bias.astype(BF).astype(F32).reshape(1, -1), row_bias.astype(BF).astype(F32).reshape(1, -1)],
        axis=1,
    )
    small_rel = from_planes(small)
    part, silu_own, ada_low = call(
        functools.partial(mod_body, G), (1,),
        [full(small.shape)] * G + [full((share, ada))],
        [full((G, ada)), full((G, share)), full((share, ada))],
        [shape((G, ada), F32), shape((G, share), BF), shape((share, ada), BF)],
        (*small_rel, w_ada), scalar=scalar, nbytes=8 * share * ada, near=True,
    )
    bias_rev = jnp.concatenate(small_rel[::-1] * 2, axis=0)[:, D:]
    bias_abs = lax.dynamic_slice_in_dim(bias_rev, G - 1 - z, G, 0)
    cols = bias_abs[:, :n_col].reshape(-1)
    bias_rows = bias_abs[:, n_col:].reshape(G, 2, share).transpose(1, 0, 2).reshape(2, D)
    bias_up = cols[ada + 2 * hc :].reshape(1, F)
    bias_qkv = jnp.stack(
        [cols[ada : ada + hc].reshape(heads, HD), jnp.zeros((heads, HD), F32),
         cols[ada + hc : ada + 2 * hc].reshape(heads, HD)], axis=1,
    ).reshape(1, 3 * hc)
    mod_part = part[0:1] + cols[:ada].reshape(1, ada)
    for k in range(1, G):
        mod_part = mod_part + around(part[k : k + 1], G - k)
    mod = lax.all_gather(mod_part, "tensor", axis=1, tiled=True).reshape(6, D)

    first_all, mod = lax.optimization_barrier((first_all, mod))
    w_qkv_all, proj_own = call(
        unpack_first_body, (1,), [full((D, 4 * hc))],
        [full((D, 3 * hc)), full((hc, D))], [shape((D, 3 * hc), BF), shape((hc, D), BF)],
        (first_all,), nbytes=20 * hc * D,
    )

    blk = min(256, S)
    steps = (S // blk,)
    wide_blk = min(1024, S)
    wide_steps = (S // wide_blk,)
    mod_in1, qkv = call(
        enter_body, steps,
        [rows_of(blk, D), full((6, D)), full((1, 3 * hc)), full((D, 3 * hc))],
        [rows_of(blk, D), rows_of(blk, 3 * hc)],
        [far_shape((S, D), BF), shape((S, 3 * hc), BF)],
        (inputs, mod, bias_qkv, w_qkv_all), flops=2 * S * D * 3 * hc, nbytes=6 * S * D,
    )
    attended, lse = call(
        attend_body, wide_steps,
        [rows_of(wide_blk, 3 * hc), full((S, 3 * hc))],
        [rows_of(wide_blk, hc), pl.BlockSpec((heads, wide_blk), lambda i: (0, i))],
        [shape((S, hc), BF), shape((heads, S), F32)],
        (qkv, qkv), flops=16 * S * S * hc, nbytes=4 * S * hc, mib=32,
    )
    if T == 8:
        proj_near, _ = lax.optimization_barrier((spread_first(proj_own, T), qkv))
        proj_more, attended = lax.optimization_barrier((spread_second(proj_near, T), attended))
        proj_all = spread_third(proj_own, proj_near, proj_more, T)
    else:
        proj_all = spread(proj_own, T)
    att_rel = spread(attended, T)
    mod_in2, branch1 = call(
        functools.partial(middle_body, T, rows), steps,
        [rows_of(blk, hc)] * T + [full((hc, D))] * T + [rows_of(blk, D), full((6, D)), full((1, D))],
        [rows_of(blk, D), full((rows, D))],
        [far_shape((S, D), BF), shape((rows, D), F32)],
        (*att_rel, *proj_all, inputs, mod, bias_rows[0:1]),
        scratch=[pltpu.VMEM((T * hc, D), BF), pltpu.VMEM((blk, D), F32)],
        scalar=scalar, flops=2 * S * D * D, nbytes=8 * S * D,
    )

    pair = 2 * rows
    pairs = (T // 2,)
    place_pair = pl.BlockSpec((1, rows, D), lambda i, s_ref: (i ^ (s_ref[0] // 2), 0, 0))
    halves = [shape((T // 2, rows, D), BF)] * 2
    activ, dpre, keep, send, keep2, send2, up_sum, down_sum, out_sum = call(
        functools.partial(mlp_body, rows), pairs,
        [rows_of(pair, D), rows_of(pair, D), full((6, D)), full((1, F))]
        + [full((G, 2 * F, share))],
        [rows_of(pair, F), rows_of(pair, F)] + [place_pair] * 4 + [full((1, F)), full((1, D)), full((1, D))],
        [far_shape((S, F), BF), far_shape((S, F), BF), *halves, *halves, shape((1, F), F32),
         shape((1, D), F32), shape((1, D), F32)],
        (mod_in2, cotangent, mod, bias_up, pack_all),
        scratch=[pltpu.VMEM((F, D), BF), pltpu.VMEM((D, F), BF)],
        scalar=scalar, flops=8 * S * D * F, nbytes=12 * S * D,
    )
    def mlp_grads(after):
        late, _ = lax.optimization_barrier((dpre, after))
        return call(
            mlp_grad_body, (G,),
            [pl.BlockSpec((S, share), lambda i: (0, i)), full((S, F)), full((S, F)),
             pl.BlockSpec((S, share), lambda i: (0, i)), pl.BlockSpec((6, share), lambda i: (0, i))],
            pl.BlockSpec((1, 2 * F, share), lambda i: (i, 0, 0)), far_shape((G, 2 * F, share), BF),
            (mod_in2, late, activ, cotangent, mod), flops=4 * S * D * F, nbytes=8 * S * D,
        )

    din2, mlp_grad = fold([keep], [send], T, mlp_grads)
    mlp_grad = lax.psum_scatter(mlp_grad.reshape(G * 2 * F, share), "dp", scatter_dimension=0, tiled=True)
    cot_rows = lax.dynamic_slice_in_dim(cotangent, t * rows, rows, 0)
    x_rows = lax.dynamic_slice_in_dim(inputs, t * rows, rows, 0)
    half = [full((1, rows, D // 2))] * 4
    own = full((rows, D))
    dres1, dbranch1, resid1, sums_mid = call(
        between_body, (1,), half + [own, full((6, D)), own, own], [own, own, own, full((3, D))],
        [far_shape((rows, D), F32), shape((rows, D), BF), far_shape((rows, D), F32), shape((3, D), F32)],
        (*din2, x_rows, mod, cot_rows, branch1), nbytes=24 * rows * D, near=True,
    )
    dbr_rel = spread(dbranch1, T)
    dqkv, qkv_sum, proj_sum, proj_grad = call(
        functools.partial(attend_back_body, T, rows), wide_steps,
        [own] * T + [full((hc, D)), full((S, 3 * hc)), pl.BlockSpec((heads, wide_blk), lambda i, *_: (0, i)),
                                         full((S, hc))],
        [full((S, 3 * hc)), full((1, 3 * hc)), full((1, D)), full((D, hc))],
        [shape((S, 3 * hc), BF), shape((1, 3 * hc), F32), shape((1, D), F32), shape((D, hc), BF)],
        (*dbr_rel, proj_own, qkv, lse, attended),
        scratch=[pltpu.VMEM((S, hc), BF), pltpu.VMEM((3 * heads, S, HD), F32)],
        scalar=scalar, flops=40 * S * S * hc, nbytes=6 * S * D,
    )
    keep1, send1, sums_in = call(
        functools.partial(leave_body, rows), pairs,
        [rows_of(pair, 3 * hc), full((D, 3 * hc)), rows_of(pair, D)],
        [place_pair, place_pair, full((2, D))],
        [far_shape((T // 2, rows, D), BF)] * 2 + [shape((2, D), F32)],
        (dqkv, w_qkv_all, inputs), scalar=scalar, flops=6 * S * D * hc, nbytes=6 * S * D, mib=32, far=(1, 2),
    )
    sums_out = out_sum + bias_rows[1:2] * jnp.sum(cot_rows.astype(F32), 0, keepdims=True)
    dmod = jnp.concatenate([sums_in, sums_mid, sums_out], axis=0).reshape(T, ada)
    dmod, mlp_grad, keep2, send2 = lax.optimization_barrier((dmod, mlp_grad, keep2, send2))
    dmod = jnp.sum(lax.all_to_all(dmod, "tensor", 0, 0, tiled=True), 0)
    wide = LR_SCALE * D ** (-0.5)
    chunks = F // share
    square = (share, share)
    up_block = pl.BlockSpec(square, lambda i: (0, i))
    down_block = pl.BlockSpec(square, lambda i: (i, 0))
    mlp_out = call(
        functools.partial(adam_mlp_body, wide, LR_SCALE * (F * T) ** (-0.5)), (chunks,),
        [down_block, pl.BlockSpec(square, lambda i: (chunks + i, 0))] + [up_block] * 3 + [down_block] * 3,
        [up_block] * 3 + [down_block] * 3,
        [far_shape((share, F), F32)] * 3 + [far_shape((F, share), F32)] * 3,
        (mlp_grad, mlp_grad, w_fc1, m_fc1, v_fc1, w_fc2, m_fc2, v_fc2), nbytes=52 * share * F,
    )
    dqkv_late, dmod, *mlp_out = lax.optimization_barrier((dqkv, dmod, *mlp_out))
    first_grad = call(
        first_grad_body, (G,),
        [pl.BlockSpec((S, share), lambda i: (0, i)), full((S, 3 * hc)), pl.BlockSpec((share, hc), lambda i: (i, 0))],
        pl.BlockSpec((share, 4 * hc), lambda i: (i, 0)), far_shape((D, 4 * hc), BF),
        (mod_in1, dqkv_late, proj_grad), flops=6 * S * D * hc, nbytes=4 * S * D, mib=32, far=(0,),
    )
    first_grad = lax.psum_scatter(first_grad, "dp", scatter_dimension=0, tiled=True)
    qkv_sum = qkv_sum.reshape(heads, 3, HD)
    message = jnp.concatenate(
        [dmod.astype(BF).astype(F32), qkv_sum[:, 0].reshape(-1), qkv_sum[:, 2].reshape(-1),
         up_sum.reshape(-1), proj_sum.reshape(-1), down_sum.reshape(-1)]
    ).reshape(1, -1)
    message_rel = jnp.concatenate(from_planes(message), axis=0)
    keep1, message_rel = lax.optimization_barrier((keep1, message_rel))
    sums, _ = fold([keep1, keep2], [send1, send2], T)
    input_grad, block_out = call(
        finish_body, (1,), [full((1, rows, D))] * 4 + [own, full((6, D)), own, full((1, D)), own], [own, own],
        [far_shape((rows, D), F32)] * 2,
        (*sums, x_rows, mod, dres1, bias_rows[1:2], resid1), nbytes=28 * rows * D, near=True, far=(6, 8),
    )
    dmod_rel = message_rel[:, :ada].astype(BF)
    bias_sum = jnp.sum(message_rel, 0)
    col_sum = lax.dynamic_slice_in_dim(bias_sum[: G * n_col], z * n_col, n_col, 0)
    row_sum = lax.dynamic_slice_in_dim(bias_sum[G * n_col :].reshape(2, D), z * share, share, 1)
    per = T // G
    grad_silu = dot(dmod_rel, ada_low, 1, 1).reshape(T, D // T)
    chunk = ada // 3
    by_chunk = pl.BlockSpec((share, chunk), lambda i: (0, i))
    ada_out = call(
        functools.partial(adam_ada_body, wide), (3,),
        [full((G, share)), pl.BlockSpec((G, chunk), lambda i: (0, i))] + [by_chunk] * 3,
        [by_chunk] * 3, [far_shape((share, ada), F32)] * 3,
        (silu_own, dmod_rel, w_ada, m_ada, v_ada), nbytes=24 * share * ada,
    )
    grad_silu, *ada_out = lax.optimization_barrier(
        (lax.all_to_all(grad_silu, "tensor", 0, 0, tiled=True), *ada_out)
    )
    grad_silu = jnp.sum(grad_silu, 0, keepdims=True)
    grad_silu = lax.ppermute(
        grad_silu, ("dp", "tensor"),
        [(a * T + b, ((a - b // per) % G) * T + a * per + b % per) for a in range(G) for b in range(T)],
    )
    cond_here = lax.dynamic_slice_in_dim(cond, t * (D // T), D // T, 1)
    sig_here = jax.nn.sigmoid(cond_here)
    cond_grad = grad_silu * sig_here * (1.0 + cond_here * (1.0 - sig_here))

    wide_block, flat = full((share, 3 * hc)), full((hc, share))
    first_out = call(
        functools.partial(adam_first_body, wide, LR_SCALE * (D // 32) ** (-0.5)), (1,),
        [full((share, 4 * hc))] + [wide_block] * 3 + [flat] * 3, [wide_block] * 3 + [flat] * 3,
        [far_shape((share, 3 * hc), F32)] * 3 + [far_shape((hc, share), F32)] * 3,
        (first_grad, w_qkv, m_qkv, v_qkv, w_proj, m_proj, v_proj), nbytes=32 * share * 4 * hc,
    )
    col_second, col_new = adam_step(col_bias, m_col, v_col, col_sum, LR_BIAS, 0.0)
    row_second, row_new = adam_step(row_bias, m_row, v_row, row_sum, LR_BIAS, 0.0)
    return (
        block_out, input_grad, cond_grad, *ada_out, *first_out, *mlp_out,
        col_sum, col_second, col_new, row_sum, row_second, row_new,
    )


def solution(mesh):
    by_cols = P("dp", "tensor")
    by_rows = P("tensor", "dp")
    column = P(("tensor", "dp"))
    row = P(None, "dp")
    tokens = P("dp", None)
    weights = (by_cols, by_cols, by_rows, by_cols, by_rows, column, row)
    moments = tuple(spec for spec in weights for _ in range(2))
    results = tuple(spec for spec in weights for _ in range(3))
    mine = P(("dp", "tensor"), None)
    return jax.shard_map(
        shards,
        mesh=mesh,
        in_specs=(tokens, tokens, tokens, *weights, *moments),
        out_specs=(mine, mine, by_cols, *results),
        check_vma=False,
    )
```
